256 devices in a mesh: ocn: 8 (over z), atm: 32 (over y, x, core).
Axes of the slice: x: 4, y: 4, z: 8, core: 2. Of those that a mesh axis runs over, the one named last changes fastest.
Arguments:
- atm_fields: bfloat16 [2048, 32, 128], P('atm'), may hold values from -6 to 6
- weights: bfloat16 [98304, 128, 128], P(('ocn', 'atm')), may hold values from -0.5 to 0.5
- surf_temp: float32 [98304, 128], P(('ocn', 'atm')), may hold values from -6 to 6
- surf_hum: float32 [98304, 128], P(('ocn', 'atm')), may hold values from -6 to 6
- roughness: float32 [98304, 128], P(('ocn', 'atm')), may hold values from 0.0001 to 0.1
- cell_area: float32 [98304, 128], P(('ocn', 'atm')), may hold values from 0.2 to 2
- need_list: int32 [256, 32, 4], P(('ocn', 'atm')), may hold values from 0 to 63
- use_slot: int32 [98304], P(('ocn', 'atm')), may hold values from 0 to 127, as said below
- ocean_block: int32 [98304], P(('ocn', 'atm')), may hold values from 0 to 31
- ocean_cell: int32 [98304, 128], P(('ocn', 'atm')), may hold values from 0 to 127
- cell_count: int32 [98304], P(('ocn', 'atm')), may hold values from 1 to 128, as said below
- ice_mask: int32 [98304, 128], P(('ocn', 'atm')), may hold values 0 or 1
Outputs:
- atm_flux: float32 [2048, 4, 128], P('atm')
- ocean_flux: float32 [256, 32, 128], P(('ocn', 'atm'))
The draws below stay inside these ranges and needn't reach their ends.
Inputs may be any that keep to these rules, and one draw needn't show every extreme that they name: `use_slot`: within the 384 exchange blocks of each device every slot value appears at least once. `cell_count`: each device has a block with 128 live cells and one with a single live cell.
All inputs are finite; a program needn't handle non-finite values. No bound on the sum of `ice_mask` on one device may be relied on, other than what follows from the above.
Results may differ from the reference program's by a relative error of at most 0.00087.
Values may be sent and summed in bfloat16 or wider, within the bound.
No kernel may reach another device: no remote copies, remote signals or barrier semaphores. Data moves between devices by JAX's collectives and lax.ppermute only.
A program may use at most 128 MiB of HBM per device.

```python
import math
import jax
import jax.numpy as jnp
from jax import lax

F = 32
BLK = 128
ACELL = 128
OCELL = 128
CAP = 4
ITERS = 8
ABD = 64
OBD = 1
XB_DEV = 384
ATM_BLOCKS = 2048
XBLOCKS = 98304
OCEAN_BLOCKS = 256
N_OCN = 8
N_ATM = 32
DEVICES = 256


def draw_use_slot(key, part):
    ndevices = N_OCN * N_ATM
    subkeys = jax.random.split(key, ndevices)
    orders = jax.vmap(lambda subkey: jax.random.permutation(subkey, XB_DEV))(subkeys)
    return (orders % (N_ATM * CAP)).astype(jnp.int32).reshape(-1)


def draw_cell_count(key, part):
    ndevices = N_OCN * N_ATM
    counts = jax.random.randint(key, (ndevices, XB_DEV), 1, BLK + 1)
    counts = counts.at[:, 0].set(BLK).at[:, 1].set(1)
    return counts.astype(jnp.int32).reshape(-1)


def with_ends(drawn, own_key, least, high):
    shape = drawn.shape
    index_at = [jax.random.randint(jax.random.fold_in(own_key, axis), (), 0, shape[axis]) for axis in range(len(shape))]
    drawn = drawn.at[tuple(index_at)].set(least)
    longest = shape.index(max(shape))
    index_at[longest] = (index_at[longest] + 1) % shape[longest]
    return drawn.at[tuple(index_at)].set(high)


def levels(rng, extent, pieces, low, high):
    def one(position, parts):
        draws = jax.random.uniform(jax.random.fold_in(jax.random.fold_in(rng, 6), position), (parts,), jnp.float32, low / len(pieces), high / len(pieces))
        return jnp.repeat(jnp.exp(draws), extent[position] // parts).reshape((-1,) + (1,) * (len(extent) - position - 1))

    factor_of = one(*pieces[0])
    for cut in pieces[1:]:
        factor_of = factor_of * one(*cut)
    return factor_of


def noise(key, dims, scale, most, pieces=(), held_as=jnp.bfloat16):
    factor_of = levels(key, dims, pieces, -0.22, 0.18) if pieces else 1.0
    entries = jax.random.normal(key, dims, jnp.float32) * scale * factor_of
    return jnp.minimum(jnp.maximum(entries, -most), most).astype(held_as)


def setup_inputs(seed: int = 0) -> dict:
    key_of = jax.random.split(jax.random.key(seed), 13)
    atm_fields = noise(key_of[0], (ATM_BLOCKS, F, ACELL), 1.0, 6.0, ((0, 32),))
    weights = noise(key_of[1], (XBLOCKS, BLK, ACELL), ACELL ** -0.5, 0.5, ((0, 256),))
    surf_temp = noise(key_of[2], (XBLOCKS, BLK), 1.0, 6.0, ((0, 256),), jnp.float32)
    surf_hum = noise(key_of[3], (XBLOCKS, BLK), 1.0, 6.0, ((0, 256),), jnp.float32)
    roughness = jnp.clip(jnp.exp(math.log(0.1) - 6.9077553 * jax.random.uniform(key_of[4], (XBLOCKS, BLK), jnp.float32) ** levels(key_of[4], (XBLOCKS, BLK), ((0, 256),), -0.2, 0.2)), 0.0001, 0.1)
    cell_area = jnp.clip(jnp.exp(math.log(2.0) - 2.3025851 * jax.random.uniform(key_of[5], (XBLOCKS, BLK), jnp.float32) ** levels(key_of[5], (XBLOCKS, BLK), ((0, 256),), -0.2, 0.2)), 0.2, 2.0)
    need_list = with_ends(jax.random.randint(key_of[6], (DEVICES, N_ATM, CAP), 0, ABD), jax.random.fold_in(key_of[6], 1), 0, ABD - 1).astype(jnp.int32)
    use_slot = draw_use_slot(jax.random.fold_in(key_of[12], 71), 0)
    ocean_block = with_ends(jax.random.randint(key_of[8], (XBLOCKS,), 0, N_ATM * OBD), jax.random.fold_in(key_of[8], 1), 0, (N_ATM * OBD) - 1).astype(jnp.int32)
    ocean_cell = with_ends(jax.random.randint(key_of[9], (XBLOCKS, BLK), 0, OCELL), jax.random.fold_in(key_of[9], 1), 0, OCELL - 1).astype(jnp.int32)
    cell_count = draw_cell_count(jax.random.fold_in(key_of[12], 71), 0)
    ice_mask = with_ends((jax.random.randint(key_of[11], (XBLOCKS, BLK), 0, 3) < 1).astype(jnp.int32), jax.random.fold_in(key_of[11], 1), 0, 1)
    return dict(atm_fields=atm_fields, weights=weights, surf_temp=surf_temp, surf_hum=surf_hum, roughness=roughness, cell_area=cell_area, need_list=need_list, use_slot=use_slot, ocean_block=ocean_block, ocean_cell=ocean_cell, cell_count=cell_count, ice_mask=ice_mask)


ref_height = 10.0
karman = 0.4
buoyancy = 0.5
flux_scale = 40.0

def similarity(wind_speed, temp_diff, hum_diff, log_mom, log_heat, psi_mom, psi_heat):
    fric_vel = karman * wind_speed / (log_mom - psi_mom)
    temp_scale = karman * temp_diff / (log_heat - psi_heat)
    hum_scale = karman * hum_diff / (log_heat - psi_heat)
    return (fric_vel, temp_scale, hum_scale)

def bulk_fluxes(mapped, surf_temp, surf_hum, roughness, ice_frac):
    wind_u = 6.0 * mapped[:, 0]
    wind_v = 6.0 * mapped[:, 1]
    wind_speed = jnp.sqrt(wind_u * wind_u + wind_v * wind_v + 1.0)
    temp_diff = mapped[:, 2] - surf_temp
    hum_diff = (mapped[:, 3] - surf_hum) * (1.0 - 0.6 * ice_frac)
    log_mom = jnp.log(ref_height / roughness)
    log_heat = log_mom + math.log(10.0)
    psi_mom = jnp.zeros_like(wind_speed)
    psi_heat = jnp.zeros_like(wind_speed)
    for sweep in range(ITERS):
        fric_vel, temp_scale, hum_scale = similarity(wind_speed, temp_diff, hum_diff, log_mom, log_heat, psi_mom, psi_heat)
        stability = jnp.clip(ref_height * karman * buoyancy * (temp_scale + 0.2 * hum_scale) / (fric_vel * fric_vel), -5.0, 1.0)
        unstable = jnp.minimum(stability, 0.0)
        root_term = jnp.sqrt(jnp.sqrt(1.0 - 16.0 * unstable))
        square_term = jnp.log((1.0 + root_term * root_term) / 2.0)
        psi_mom = jnp.where(stability >= 0.0, -5.0 * stability, 2.0 * jnp.log((1.0 + root_term) / 2.0) + square_term - 2.0 * jnp.arctan(root_term) + math.pi / 2.0)
        psi_heat = jnp.where(stability >= 0.0, -5.0 * stability, 2.0 * square_term)
    fric_vel, temp_scale, hum_scale = similarity(wind_speed, temp_diff, hum_diff, log_mom, log_heat, psi_mom, psi_heat)
    return jnp.stack([flux_scale * fric_vel * fric_vel * wind_u / wind_speed, flux_scale * fric_vel * fric_vel * wind_v / wind_speed, -flux_scale * fric_vel * temp_scale, -flux_scale * fric_vel * hum_scale], axis=1)

def reference(atm_fields, weights, surf_temp, surf_hum, roughness, cell_area, need_list, use_slot, ocean_block, ocean_cell, cell_count, ice_mask):
    ndevices = N_OCN * N_ATM

    def per_device(inputs):
        wblock, stemp, shum, rough, area, need, slot, oblock, ocell, count, ice = inputs
        owner = slot // CAP
        column = slot % CAP
        source = (owner * ABD + need[owner, column]).astype(jnp.int32)
        picked = atm_fields[source]
        mapped = jnp.einsum('kfa,kba->kfb', picked.astype(jnp.float32), wblock.astype(jnp.float32))
        ice_frac = ice.astype(jnp.float32)
        flux4 = bulk_fluxes(mapped, stemp, shum, rough, ice_frac)
        is_live = (jnp.arange(BLK, dtype=jnp.int32)[None, :] < count[:, None]).astype(jnp.float32)
        cell_weight = area * is_live
        weighted = (cell_weight[:, None, :] * flux4).astype(jnp.bfloat16)
        contrib = jnp.einsum('kcb,kba->kca', weighted.astype(jnp.float32), wblock.astype(jnp.float32))
        passive = mapped[:, 4:] * (1.0 - 0.7 * ice_frac)[:, None, :]
        ocean_values = cell_weight[:, None, :] * jnp.concatenate([flux4, passive], axis=1)
        cell_hot = (ocell[:, :, None] == jnp.arange(OCELL, dtype=jnp.int32)[None, None, :]).astype(jnp.float32)
        partial_sum = jnp.einsum('kfb,kbc->kfc', ocean_values, cell_hot, precision=lax.Precision.HIGHEST)
        picker = (oblock[None, :] == jnp.arange(N_ATM * OBD, dtype=jnp.int32)[:, None]).astype(jnp.float32)
        row_term = jnp.dot(picker, partial_sum.reshape(XB_DEV, F * OCELL), precision=lax.Precision.HIGHEST)
        return (contrib, source, row_term)
    inputs = (weights.reshape(ndevices, XB_DEV, BLK, ACELL), surf_temp.reshape(ndevices, XB_DEV, BLK), surf_hum.reshape(ndevices, XB_DEV, BLK), roughness.reshape(ndevices, XB_DEV, BLK), cell_area.reshape(ndevices, XB_DEV, BLK), need_list, use_slot.reshape(ndevices, XB_DEV), ocean_block.reshape(ndevices, XB_DEV), ocean_cell.reshape(ndevices, XB_DEV, BLK), cell_count.reshape(ndevices, XB_DEV), ice_mask.reshape(ndevices, XB_DEV, BLK))
    contribs, sources, terms = lax.map(per_device, inputs)
    atm_flux = jax.ops.segment_sum(contribs.reshape(ndevices * XB_DEV, 4, ACELL), sources.reshape(ndevices * XB_DEV), num_segments=ATM_BLOCKS)
    ocean_flux = lax.optimization_barrier(jnp.sum(terms.reshape(N_OCN, N_ATM, N_ATM * OBD, F * OCELL), axis=1)).reshape(OCEAN_BLOCKS, F, OCELL)
    return (atm_flux, ocean_flux)
```

```python
import math

import jax
import jax.numpy as jnp
from jax import lax
from jax.experimental import pallas as pl
from jax.experimental.pallas import tpu as pltpu
from jax.sharding import PartitionSpec as P

F = 32
BLK = 128
ACELL = 128
OCELL = 128
CAP = 4
ITERS = 8

ref_height = 10.0
karman = 0.4
buoyancy = 0.5
flux_scale = 40.0

CHUNK = 64
GROUP = 8
MIB = 1 << 20
VMEM = pltpu.VMEM
SMEM = pltpu.SMEM

ARCTAN = (
    0.9999999952,
    -0.3333319239,
    0.1999324926,
    -0.1416585733,
    0.1012280370,
    -0.0507783010,
)


def arctan_half(t):
    z = t * t
    total = jnp.full_like(z, ARCTAN[-1])
    for c in ARCTAN[-2::-1]:
        total = total * z + c
    return total * t


def flux_rows(mapped_u, mapped_v, mapped_t, mapped_q, surf_temp, surf_hum, hum_factor, log_mom):
    wind_u = 6.0 * mapped_u
    wind_v = 6.0 * mapped_v
    square_speed = wind_u * wind_u + wind_v * wind_v + 1.0
    wind_speed = jnp.sqrt(square_speed)
    temp_diff = mapped_t - surf_temp
    hum_diff = (mapped_q - surf_hum) * hum_factor
    log_heat = log_mom + math.log(10.0)
    gain = (ref_height * buoyancy) * (temp_diff + 0.2 * hum_diff) / square_speed
    from_mom = log_mom
    from_heat = log_heat
    for sweep in range(ITERS):
        stability = jnp.clip(gain * from_mom * from_mom / from_heat, -5.0, 1.0)
        unstable = jnp.minimum(stability, 0.0)
        square = jnp.sqrt(1.0 - 16.0 * unstable)
        root = jnp.sqrt(square)
        half_square = 0.5 + 0.5 * square
        half_root = 0.5 + 0.5 * root
        log_square = jnp.log(half_square)
        log_both = jnp.log(half_root * half_root * half_square)
        turn = arctan_half((root - 1.0) / (root + 1.0))
        stable = stability >= 0.0
        psi_stable = -5.0 * stability
        psi_mom = jnp.where(stable, psi_stable, log_both - 2.0 * turn)
        psi_heat = jnp.where(stable, psi_stable, 2.0 * log_square)
        from_mom = log_mom - psi_mom
        from_heat = log_heat - psi_heat
    fric_vel = karman * wind_speed / from_mom
    drag = flux_scale * fric_vel * fric_vel / wind_speed
    carry = -flux_scale * karman * fric_vel / from_heat
    return drag * wind_u, drag * wind_v, carry * temp_diff, carry * hum_diff


def serve_body(requests, fields, out):
    def owner(d, _):
        for c in range(CAP):
            out[d * CAP + c] = fields[requests[d, c]]
        return 0

    lax.fori_loop(0, out.shape[0] // CAP, owner, 0)


def serve(requests, fields):
    return pl.pallas_call(
        serve_body,
        out_shape=jax.ShapeDtypeStruct((requests.size,) + fields.shape[1:], fields.dtype),
        in_specs=[pl.BlockSpec(memory_space=SMEM), pl.BlockSpec(memory_space=VMEM)],
        out_specs=pl.BlockSpec(memory_space=VMEM),
        compiler_params=pltpu.CompilerParams(vmem_limit_bytes=8 * MIB),
        name="serve",
    )(requests, fields)


def couple_body(
    use_slot,
    ocean_block,
    table,
    weights,
    surf_temp,
    surf_hum,
    hum_factor,
    log_mom,
    cell_weight,
    passive_weight,
    ocean_cell,
    slot_sums,
    ocean_sums,
    rows,
):
    step = pl.program_id(0)

    @pl.when(step == 0)
    def _():
        slot_sums[...] = jnp.zeros_like(slot_sums)
        ocean_sums[...] = jnp.zeros_like(ocean_sums)

    first = step * CHUNK

    def map_group(g, _):
        for i in range(GROUP):
            k = g * GROUP + i
            rows[pl.ds(pl.multiple_of(k * F, F), F), :] = lax.dot_general(
                table[use_slot[first + k]],
                weights[k],
                (((1,), (1,)), ((), ())),
                preferred_element_type=jnp.float32,
            )
        return 0

    lax.fori_loop(0, CHUNK // GROUP, map_group, 0)

    fluxes = flux_rows(
        *(rows[pl.ds(f, CHUNK, stride=F), :] for f in range(4)),
        surf_temp[...],
        surf_hum[...],
        hum_factor[...],
        log_mom[...],
    )
    for f in range(4):
        rows[pl.ds(f, CHUNK, stride=F), :] = cell_weight[...] * fluxes[f]

    cells = lax.broadcasted_iota(jnp.int32, (OCELL, BLK), 0)
    field = lax.broadcasted_iota(jnp.int32, (F, BLK), 0)

    def sum_group(g, _):
        for i in range(GROUP):
            k = g * GROUP + i
            value = rows[pl.ds(pl.multiple_of(k * F, F), F), :]
            value = jnp.where(field < 4, value, value * passive_weight[pl.ds(k, 1), :])
            high = value.astype(jnp.bfloat16)
            low = (value - high.astype(jnp.float32)).astype(jnp.bfloat16)
            contrib = jnp.dot(high[:16], weights[k], preferred_element_type=jnp.float32)
            slot = use_slot[first + k]
            slot_sums[slot] = slot_sums[slot] + contrib[:4]
            hot = jnp.where(cells == ocean_cell[pl.ds(k, 1), :], 1.0, 0.0).astype(jnp.bfloat16)
            both = lax.dot_general(
                jnp.concatenate([high, low], axis=0),
                hot,
                (((1,), (1,)), ((), ())),
                preferred_element_type=jnp.float32,
            )
            target = ocean_block[first + k]
            ocean_sums[target] = ocean_sums[target] + (both[:F] + both[F:])
        return 0

    lax.fori_loop(0, CHUNK // GROUP, sum_group, 0)


def couple(use_slot, ocean_block, table, weights, cells, ocean_cell, owners):
    blocks = weights.shape[0]
    whole = lambda shape: pl.BlockSpec(shape, lambda s, *_: (0,) * len(shape))
    part = pl.BlockSpec((CHUNK, BLK), lambda s, *_: (s, 0))
    return pl.pallas_call(
        couple_body,
        out_shape=(
            jax.ShapeDtypeStruct((table.shape[0], 4, ACELL), jnp.float32),
            jax.ShapeDtypeStruct((owners, F, OCELL), jnp.float32),
        ),
        grid_spec=pltpu.PrefetchScalarGridSpec(
            num_scalar_prefetch=2,
            grid=(blocks // CHUNK,),
            in_specs=[
                whole(table.shape),
                pl.BlockSpec((CHUNK, BLK, ACELL), lambda s, *_: (s, 0, 0)),
            ]
            + [part] * 7,
            out_specs=(whole((table.shape[0], 4, ACELL)), whole((owners, F, OCELL))),
            scratch_shapes=[pltpu.VMEM((CHUNK * F, BLK), jnp.float32)],
        ),
        compiler_params=pltpu.CompilerParams(vmem_limit_bytes=32 * MIB),
        name="couple",
    )(use_slot, ocean_block, table, weights, *cells, ocean_cell)


def gather_sums_body(place, requests, returned, *rest):
    outs, sums = rest[:-1], rest[-1]
    sums[...] = jnp.zeros_like(sums)

    def owner(d, _):
        for c in range(CAP):
            b = requests[d, c]
            sums[b] = sums[b] + returned[d * CAP + c]
        return 0

    lax.fori_loop(0, returned.shape[0] // CAP, owner, 0)
    ranks = len(outs)
    share = sums.shape[0] // ranks
    for s in range(ranks):
        out_of = lax.rem(place[0] + s, ranks)
        outs[s][...] = sums[pl.ds(out_of * share, share)]


def gather_sums(place, requests, returned, local_blocks, ranks):
    share = (local_blocks // ranks,) + returned.shape[1:]
    return pl.pallas_call(
        gather_sums_body,
        out_shape=[jax.ShapeDtypeStruct(share, jnp.float32)] * ranks,
        in_specs=[
            pl.BlockSpec(memory_space=SMEM),
            pl.BlockSpec(memory_space=SMEM),
            pl.BlockSpec(memory_space=VMEM),
        ],
        out_specs=[pl.BlockSpec(memory_space=VMEM)] * ranks,
        scratch_shapes=[pltpu.VMEM((local_blocks,) + returned.shape[1:], jnp.float32)],
        compiler_params=pltpu.CompilerParams(vmem_limit_bytes=8 * MIB),
        name="gather_sums",
    )(place, requests, returned)


def lay_out_body(place, *rest):
    parts, out = rest[:-1], rest[-1]
    ranks = len(parts)
    share = out.shape[0] // ranks
    for s in range(ranks):
        owner = lax.rem(place[0] + (ranks - s), ranks)
        out[pl.ds(owner * share, share)] = parts[s][...]


def lay_out(place, parts):
    ranks = len(parts)
    shape = (parts[0].shape[0] * ranks,) + parts[0].shape[1:]
    return pl.pallas_call(
        lay_out_body,
        out_shape=jax.ShapeDtypeStruct(shape, jnp.float32),
        in_specs=[pl.BlockSpec(memory_space=SMEM)] + [pl.BlockSpec(memory_space=VMEM)] * ranks,
        out_specs=pl.BlockSpec(memory_space=VMEM),
        compiler_params=pltpu.CompilerParams(vmem_limit_bytes=8 * MIB),
        name="lay_out",
    )(place, *parts)


def shift(x, axis, by):
    ranks = lax.axis_size(axis)
    return lax.ppermute(x, axis, [(i, (i + by) % ranks) for i in range(ranks)])


def per_device(
    atm_fields,
    weights,
    surf_temp,
    surf_hum,
    roughness,
    cell_area,
    need_list,
    use_slot,
    ocean_block,
    ocean_cell,
    cell_count,
    ice_mask,
):
    owners = lax.axis_size("atm")
    ranks = lax.axis_size("ocn")
    local_blocks = atm_fields.shape[0]
    place = lax.axis_index("ocn").astype(jnp.int32).reshape(1)
    requests = lax.all_to_all(need_list[0], "atm", split_axis=0, concat_axis=0, tiled=True)
    table = lax.all_to_all(serve(requests, atm_fields), "atm", split_axis=0, concat_axis=0, tiled=True)
    ice_frac = ice_mask.astype(jnp.float32)
    is_live = jnp.arange(BLK, dtype=jnp.int32)[None, :] < cell_count[:, None]
    cell_weight = jnp.where(is_live, cell_area, 0.0)
    cells = (
        surf_temp,
        surf_hum,
        1.0 - 0.6 * ice_frac,
        jnp.log(ref_height / roughness),
        cell_weight,
        cell_weight * (1.0 - 0.7 * ice_frac),
    )
    slot_sums, ocean_sums = couple(
        use_slot, ocean_block, table, weights, cells, ocean_cell, owners
    )
    returned = lax.all_to_all(slot_sums, "atm", split_axis=0, concat_axis=0, tiled=True)
    ocean_parts = lax.all_to_all(ocean_sums, "atm", split_axis=0, concat_axis=0, tiled=True)
    shares = gather_sums(place, requests, returned, local_blocks, ranks)
    mine = shares[0]
    for s in range(1, ranks):
        mine = mine + shift(shares[s], "ocn", s)
    atm_flux = lay_out(place, [mine] + [shift(mine, "ocn", s) for s in range(1, ranks)])
    ocean_flux = jnp.sum(ocean_parts, axis=0, keepdims=True)
    return (atm_flux, ocean_flux)


def solution(mesh):
    placed = (
        P("atm", None, None),
        P(("ocn", "atm"), None, None),
        P(("ocn", "atm"), None),
        P(("ocn", "atm"), None),
        P(("ocn", "atm"), None),
        P(("ocn", "atm"), None),
        P(("ocn", "atm"), None, None),
        P(("ocn", "atm")),
        P(("ocn", "atm")),
        P(("ocn", "atm"), None),
        P(("ocn", "atm")),
        P(("ocn", "atm"), None),
    )
    return jax.shard_map(
        per_device,
        mesh=mesh,
        in_specs=placed,
        out_specs=(P("atm", None, None), P(("ocn", "atm"), None, None)),
        check_vma=False,
    )
```

```python
import math

import jax
import jax.numpy as jnp
from jax import lax
from jax.experimental import pallas as pl
from jax.experimental.pallas import tpu as pltpu
from jax.sharding import PartitionSpec as P

F = 32
BLK = 128
ACELL = 128
OCELL = 128
CAP = 4
ITERS = 8

ref_height = 10.0
karman = 0.4
buoyancy = 0.5
flux_scale = 40.0

GROUP = 64
FLUX_ROWS = 64
PARTS = 6
MIB = 1 << 20
VMEM = pltpu.VMEM
SMEM = pltpu.SMEM

ARCTAN = (
    0.9999999952,
    -0.3333319239,
    0.1999324926,
    -0.1416585733,
    0.1012280370,
    -0.0507783010,
)


def arctan_half(t):
    z = t * t
    total = jnp.full_like(z, ARCTAN[-1])
    for c in ARCTAN[-2::-1]:
        total = total * z + c
    return total * t


def flux_rows(mapped_u, mapped_v, mapped_t, mapped_q, surf_temp, surf_hum, hum_factor, log_mom):
    wind_u = 6.0 * mapped_u
    wind_v = 6.0 * mapped_v
    square_speed = wind_u * wind_u + wind_v * wind_v + 1.0
    wind_speed = jnp.sqrt(square_speed)
    temp_diff = mapped_t - surf_temp
    hum_diff = (mapped_q - surf_hum) * hum_factor
    log_heat = log_mom + math.log(10.0)
    gain = (ref_height * buoyancy) * (temp_diff + 0.2 * hum_diff) / square_speed
    from_mom = log_mom
    from_heat = log_heat
    for sweep in range(ITERS):
        stability = jnp.clip(gain * from_mom * from_mom / from_heat, -5.0, 1.0)
        unstable = jnp.minimum(stability, 0.0)
        square = jnp.sqrt(1.0 - 16.0 * unstable)
        root = jnp.sqrt(square)
        half_square = 0.5 + 0.5 * square
        half_root = 0.5 + 0.5 * root
        log_square = jnp.log(half_square)
        log_both = jnp.log(half_root * half_root * half_square)
        turn = arctan_half((root - 1.0) / (root + 1.0))
        stable = stability >= 0.0
        psi_stable = -5.0 * stability
        psi_mom = jnp.where(stable, psi_stable, log_both - 2.0 * turn)
        psi_heat = jnp.where(stable, psi_stable, 2.0 * log_square)
        from_mom = log_mom - psi_mom
        from_heat = log_heat - psi_heat
    fric_vel = karman * wind_speed / from_mom
    drag = flux_scale * fric_vel * fric_vel / wind_speed
    carry = -flux_scale * karman * fric_vel / from_heat
    return drag * wind_u, drag * wind_v, carry * temp_diff, carry * hum_diff


def serve_body(requests, fields, out):
    def owner(d, _):
        for c in range(CAP):
            out[d * CAP + c] = fields[requests[d, c]]
        return 0

    lax.fori_loop(0, out.shape[0] // CAP, owner, 0)


def serve(requests, fields):
    return pl.pallas_call(
        serve_body,
        out_shape=jax.ShapeDtypeStruct((requests.size,) + fields.shape[1:], fields.dtype),
        in_specs=[pl.BlockSpec(memory_space=SMEM), pl.BlockSpec(memory_space=VMEM)],
        out_specs=pl.BlockSpec(memory_space=VMEM),
        compiler_params=pltpu.CompilerParams(vmem_limit_bytes=8 * MIB),
        name="serve",
    )(requests, fields)


def prep_body(weights, ocean_cell, surf_temp, surf_hum, held, turned, hot, temp, hum, cells, sem, part_sem):
    small = [
        pltpu.make_async_copy(ocean_cell, cells, sem.at[0]),
        pltpu.make_async_copy(surf_temp, temp, sem.at[1]),
        pltpu.make_async_copy(surf_hum, hum, sem.at[2]),
    ]
    blocks = held.shape[0]
    share = blocks // PARTS
    large = [
        pltpu.make_async_copy(
            weights.at[pl.ds(p * share, share)], held.at[pl.ds(p * share, share)], part_sem.at[p]
        )
        for p in range(PARTS)
    ]
    for copy in small + large:
        copy.start()
    small[0].wait()
    target = lax.broadcasted_iota(jnp.int32, (OCELL, BLK), 0)

    def spread(g, _):
        first = pl.multiple_of(g * 16, 16)
        rows = cells[pl.ds(first, 16), :]
        for i in range(16):
            hot[first + i] = jnp.where(target == rows[i : i + 1], 1.0, 0.0).astype(jnp.bfloat16).T
        return 0

    lax.fori_loop(0, blocks // 16, spread, 0)
    for p in range(PARTS):
        large[p].wait()

        def turn(g, _):
            first = p * share + g * 16
            for i in range(16):
                turned[first + i] = held[first + i].T
            return 0

        lax.fori_loop(0, share // 16, turn, 0)
    small[1].wait()
    small[2].wait()


def prep(weights, ocean_cell, surf_temp, surf_hum):
    blocks = weights.shape[0]
    square = pltpu.VMEM((blocks, BLK, ACELL), jnp.bfloat16)
    flat = pltpu.VMEM(surf_temp.shape, jnp.float32)
    return pl.pallas_call(
        prep_body,
        out_shape=(square, square, square, flat, flat),
        in_specs=[pl.BlockSpec(memory_space=pltpu.HBM)] * 4,
        out_specs=(pl.BlockSpec(memory_space=VMEM),) * 5,
        scratch_shapes=[
            pltpu.VMEM(ocean_cell.shape, jnp.int32),
            pltpu.SemaphoreType.DMA((3,)),
            pltpu.SemaphoreType.DMA((PARTS,)),
        ],
        compiler_params=pltpu.CompilerParams(vmem_limit_bytes=4 * MIB),
        cost_estimate=pl.CostEstimate(
            flops=2 * weights.size, bytes_accessed=4 * weights.size, transcendentals=0
        ),
        name="prep",
    )(weights, ocean_cell, surf_temp, surf_hum)


def two_parts(value):
    high = value.astype(jnp.bfloat16)
    return high, (value - high.astype(jnp.float32)).astype(jnp.bfloat16)


def product(left, right):
    return jnp.dot(left, right, preferred_element_type=jnp.float32)


def sum_rows(picked, values, out, stride):
    entries = picked.shape[1]
    for c in range(4):
        high, low = two_parts(values[pl.ds(c, entries, stride=stride), :])
        out[pl.ds(c, picked.shape[0], stride=4), :] = product(picked, high) + product(picked, low)


def one_hot(index_row, count):
    rows = lax.broadcasted_iota(jnp.int32, (count, index_row.shape[1]), 0)
    return jnp.where(rows == index_row, 1.0, 0.0).astype(jnp.bfloat16)


def flux_body(
    use_slot,
    slot_row,
    table,
    turned,
    held,
    surf_temp,
    surf_hum,
    hum_factor,
    log_mom,
    cell_weight,
    rows,
    slot_sums,
    contrib,
):
    blocks = held.shape[0]

    def map_group(g, _):
        base = g * GROUP
        for i in range(0, GROUP, 2):
            k = base + i
            both = product(
                jnp.concatenate([table[use_slot[k]], table[use_slot[k + 1]]], axis=0),
                jnp.concatenate([turned[k], turned[k + 1]], axis=1),
            )
            rows[pl.ds(pl.multiple_of(k * F, F), F), :] = both[:F, :BLK]
            rows[pl.ds(pl.multiple_of(k * F + F, F), F), :] = both[F:, BLK:]
        return 0

    lax.fori_loop(0, blocks // GROUP, map_group, 0)

    def iterate(g, _):
        mine = pl.ds(pl.multiple_of(g * FLUX_ROWS, FLUX_ROWS), FLUX_ROWS)
        row = lambda f: pl.ds(g * (FLUX_ROWS * F) + f, FLUX_ROWS, stride=F)
        fluxes = flux_rows(
            *(rows[row(f), :] for f in range(4)),
            surf_temp[mine, :],
            surf_hum[mine, :],
            hum_factor[mine, :],
            log_mom[mine, :],
        )
        weight = cell_weight[mine, :]
        for f in range(4):
            rows[row(f), :] = weight * fluxes[f]
        return 0

    lax.fori_loop(0, blocks // FLUX_ROWS, iterate, 0)

    def contribute(g, _):
        base = g * GROUP
        for i in range(0, GROUP, 2):
            k = base + i
            left = jnp.concatenate(
                [
                    rows[pl.ds(pl.multiple_of(k * F, F), 8), :],
                    rows[pl.ds(pl.multiple_of(k * F + F, F), 8), :],
                ],
                axis=0,
            ).astype(jnp.bfloat16)
            both = product(left, jnp.concatenate([held[k], held[k + 1]], axis=1))
            contrib[pl.ds(pl.multiple_of(k * 8, 8), 8), :] = both[:8, :ACELL]
            contrib[pl.ds(pl.multiple_of(k * 8 + 8, 8), 8), :] = both[8:, ACELL:]
        return 0

    lax.fori_loop(0, blocks // GROUP, contribute, 0)
    sum_rows(one_hot(slot_row[...], table.shape[0]), contrib, slot_sums, 8)


def fluxes_of(use_slot, table, turned, held, temp, hum, cells):
    blocks = held.shape[0]
    here = pl.BlockSpec(memory_space=VMEM)
    pinned = [pltpu.with_memory_space_constraint(x, VMEM) for x in (turned, held, temp, hum)]
    return pl.pallas_call(
        flux_body,
        out_shape=(
            pltpu.VMEM((blocks * F, BLK), jnp.float32),
            jax.ShapeDtypeStruct((table.shape[0] * 4, ACELL), jnp.float32),
        ),
        in_specs=[pl.BlockSpec(memory_space=SMEM)] + [here] * 9,
        out_specs=(here, here),
        scratch_shapes=[pltpu.VMEM((blocks * 8, ACELL), jnp.float32)],
        compiler_params=pltpu.CompilerParams(vmem_limit_bytes=8 * MIB),
        name="fluxes",
    )(use_slot, use_slot.reshape(1, -1), table, *pinned, *cells)


def ocean_body(ocean_block, rows, hot, passive_weight, ocean_sums, partial):
    ocean_sums[...] = jnp.zeros_like(ocean_sums)
    is_flux = lax.broadcasted_iota(jnp.int32, (8, BLK), 0) < 4

    def group(g, _):
        base = g * GROUP
        for i in range(GROUP):
            k = base + i
            factor = passive_weight[pl.ds(k, 1), :]
            value = rows[pl.ds(pl.multiple_of(k * F, F), F), :]
            value = jnp.concatenate(
                [jnp.where(is_flux, value[:8], value[:8] * factor), value[8:] * factor], axis=0
            )
            both = product(jnp.concatenate(two_parts(value), axis=0), hot[k])
            partial[i * F : (i + 1) * F, :] = both[:F] + both[F:]
        for i in range(GROUP):
            target = ocean_block[base + i]
            ocean_sums[target] = ocean_sums[target] + partial[i * F : (i + 1) * F, :]
        return 0

    lax.fori_loop(0, rows.shape[0] // F // GROUP, group, 0)


def ocean_of(ocean_block, rows, hot, passive_weight, owners):
    here = pl.BlockSpec(memory_space=VMEM)
    pinned = [pltpu.with_memory_space_constraint(x, VMEM) for x in (rows, hot)]
    return pl.pallas_call(
        ocean_body,
        out_shape=jax.ShapeDtypeStruct((owners, F, OCELL), jnp.float32),
        in_specs=[pl.BlockSpec(memory_space=SMEM)] + [here] * 3,
        out_specs=here,
        scratch_shapes=[pltpu.VMEM((GROUP * F, OCELL), jnp.float32)],
        compiler_params=pltpu.CompilerParams(vmem_limit_bytes=8 * MIB),
        cost_estimate=pl.CostEstimate(
            flops=128 * rows.size, bytes_accessed=12 * rows.size, transcendentals=0
        ),
        name="ocean",
    )(ocean_block, *pinned, passive_weight)


def owner_body(request_row, returned, out):
    sum_rows(one_hot(request_row[...], out.shape[0] // 4), returned, out, 4)


def owner_sums_of(requests, returned, local_blocks):
    here = pl.BlockSpec(memory_space=VMEM)
    return pl.pallas_call(
        owner_body,
        out_shape=jax.ShapeDtypeStruct((local_blocks * 4, ACELL), jnp.float32),
        in_specs=[here, here],
        out_specs=here,
        compiler_params=pltpu.CompilerParams(vmem_limit_bytes=8 * MIB),
        name="owner_sums",
    )(requests.reshape(1, -1), returned)


def sum_over(x, axis):
    ranks = lax.axis_size(axis)
    bit = 1
    while bit < ranks:
        x = x + lax.ppermute(x, axis, [(i, i ^ bit) for i in range(ranks)])
        bit *= 2
    return x


def per_device(
    atm_fields,
    weights,
    surf_temp,
    surf_hum,
    roughness,
    cell_area,
    need_list,
    use_slot,
    ocean_block,
    ocean_cell,
    cell_count,
    ice_mask,
):
    owners = lax.axis_size("atm")
    local_blocks = atm_fields.shape[0]
    requests = lax.all_to_all(need_list[0], "atm", split_axis=0, concat_axis=0, tiled=True)
    table = lax.all_to_all(serve(requests, atm_fields), "atm", split_axis=0, concat_axis=0, tiled=True)
    held, turned, hot, temp, hum = prep(weights, ocean_cell, surf_temp, surf_hum)
    ice_frac = ice_mask.astype(jnp.float32)
    is_live = jnp.arange(BLK, dtype=jnp.int32)[None, :] < cell_count[:, None]
    cell_weight = jnp.where(is_live, cell_area, 0.0)
    cells = (1.0 - 0.6 * ice_frac, jnp.log(ref_height / roughness), cell_weight)
    passive_weight = cell_weight * (1.0 - 0.7 * ice_frac)
    rows, slot_sums = fluxes_of(use_slot, table, turned, held, temp, hum, cells)
    returned = lax.all_to_all(slot_sums, "atm", split_axis=0, concat_axis=0, tiled=True)
    ocean_sums = ocean_of(ocean_block, rows, hot, passive_weight, owners)
    ocean_parts = lax.all_to_all(ocean_sums, "atm", split_axis=0, concat_axis=0, tiled=True)
    owner_sums = owner_sums_of(requests, returned, local_blocks)
    atm_flux = sum_over(owner_sums, "ocn").reshape(local_blocks, 4, ACELL)
    ocean_flux = jnp.sum(ocean_parts, axis=0, keepdims=True)
    return (atm_flux, ocean_flux)


def solution(mesh):
    placed = (
        P("atm", None, None),
        P(("ocn", "atm"), None, None),
        P(("ocn", "atm"), None),
        P(("ocn", "atm"), None),
        P(("ocn", "atm"), None),
        P(("ocn", "atm"), None),
        P(("ocn", "atm"), None, None),
        P(("ocn", "atm")),
        P(("ocn", "atm")),
        P(("ocn", "atm"), None),
        P(("ocn", "atm")),
        P(("ocn", "atm"), None),
    )
    return jax.shard_map(
        per_device,
        mesh=mesh,
        in_specs=placed,
        out_specs=(P("atm", None, None), P(("ocn", "atm"), None, None)),
        check_vma=False,
    )
```

```python
import math

import jax
import jax.numpy as jnp
from jax import lax
from jax.experimental import pallas as pl
from jax.experimental.pallas import tpu as pltpu
from jax.sharding import PartitionSpec as P

F = 32
BLK = 128
ACELL = 128
OCELL = 128
CAP = 4
ITERS = 8

ref_height = 10.0
karman = 0.4
buoyancy = 0.5
flux_scale = 40.0

GROUP = 64
MIB = 1 << 20
VMEM = pltpu.VMEM
SMEM = pltpu.SMEM

ARCTAN = (
    0.9999999952,
    -0.3333319239,
    0.1999324926,
    -0.1416585733,
    0.1012280370,
    -0.0507783010,
)


def arctan_half(t):
    z = t * t
    total = jnp.full_like(z, ARCTAN[-1])
    for c in ARCTAN[-2::-1]:
        total = total * z + c
    return total * t


def flux_rows(mapped_u, mapped_v, mapped_t, mapped_q, surf_temp, surf_hum, hum_factor, log_mom):
    wind_u = 6.0 * mapped_u
    wind_v = 6.0 * mapped_v
    square_speed = wind_u * wind_u + wind_v * wind_v + 1.0
    wind_speed = jnp.sqrt(square_speed)
    temp_diff = mapped_t - surf_temp
    hum_diff = (mapped_q - surf_hum) * hum_factor
    log_heat = log_mom + math.log(10.0)
    gain = (ref_height * buoyancy) * (temp_diff + 0.2 * hum_diff) / square_speed
    from_mom = log_mom
    from_heat = log_heat
    for sweep in range(ITERS):
        stability = jnp.clip(gain * from_mom * from_mom / from_heat, -5.0, 1.0)
        unstable = jnp.minimum(stability, 0.0)
        square = jnp.sqrt(1.0 - 16.0 * unstable)
        root = jnp.sqrt(square)
        half_square = 0.5 + 0.5 * square
        half_root = 0.5 + 0.5 * root
        log_square = jnp.log(half_square)
        log_both = jnp.log(half_root * half_root * half_square)
        turn = arctan_half((root - 1.0) / (root + 1.0))
        stable = stability >= 0.0
        psi_stable = -5.0 * stability
        psi_mom = jnp.where(stable, psi_stable, log_both - 2.0 * turn)
        psi_heat = jnp.where(stable, psi_stable, 2.0 * log_square)
        from_mom = log_mom - psi_mom
        from_heat = log_heat - psi_heat
    fric_vel = karman * wind_speed / from_mom
    drag = flux_scale * fric_vel * fric_vel / wind_speed
    carry = -flux_scale * karman * fric_vel / from_heat
    return drag * wind_u, drag * wind_v, carry * temp_diff, carry * hum_diff


def serve_body(requests, fields, out):
    def owner(d, _):
        for c in range(CAP):
            out[d * CAP + c] = fields[requests[d, c]]
        return 0

    lax.fori_loop(0, out.shape[0] // CAP, owner, 0)


def serve(requests, fields):
    return pl.pallas_call(
        serve_body,
        out_shape=jax.ShapeDtypeStruct((requests.size,) + fields.shape[1:], fields.dtype),
        in_specs=[pl.BlockSpec(memory_space=SMEM), pl.BlockSpec(memory_space=VMEM)],
        out_specs=pl.BlockSpec(memory_space=VMEM),
        compiler_params=pltpu.CompilerParams(vmem_limit_bytes=8 * MIB),
        name="serve",
    )(requests, fields)


def prep_body(ocean_cell, surf_temp, surf_hum, requests, hot, temp, hum, request_row):
    request_row[...] = requests[...]
    temp[...] = surf_temp[...]
    hum[...] = surf_hum[...]
    target = lax.broadcasted_iota(jnp.int32, (OCELL, BLK), 0)
    for i in range(hot.shape[0]):
        hot[i] = jnp.where(target == ocean_cell[i : i + 1, :], 1.0, 0.0).astype(jnp.bfloat16).T


def prep(ocean_cell, surf_temp, surf_hum, requests):
    blocks = ocean_cell.shape[0]
    part = pl.BlockSpec((GROUP, BLK), lambda s: (s, 0))
    flat = jax.ShapeDtypeStruct((blocks, BLK), jnp.float32)
    line = pl.BlockSpec((1, requests.size), lambda s: (0, 0))
    return pl.pallas_call(
        prep_body,
        out_shape=(pltpu.HBM((blocks, BLK, OCELL), jnp.bfloat16), flat, flat, jax.ShapeDtypeStruct((1, requests.size), jnp.int32)),
        grid=(blocks // GROUP,),
        in_specs=[part] * 3 + [line],
        out_specs=(pl.BlockSpec((GROUP, BLK, OCELL), lambda s: (s, 0, 0)), part, part, line),
        compiler_params=pltpu.CompilerParams(vmem_limit_bytes=16 * MIB),
        cost_estimate=pl.CostEstimate(
            flops=2 * blocks * BLK * OCELL,
            bytes_accessed=2 * blocks * BLK * OCELL,
            transcendentals=0,
        ),
        name="prep",
    )(ocean_cell, surf_temp, surf_hum, requests.reshape(1, -1))


def two_parts(value):
    high = value.astype(jnp.bfloat16)
    return high, (value - high.astype(jnp.float32)).astype(jnp.bfloat16)


def product(left, right):
    return jnp.dot(left, right, preferred_element_type=jnp.float32)


def sum_rows(picked, values, out, stride):
    entries = picked.shape[1]
    for c in range(4):
        high, low = two_parts(values[pl.ds(c, entries, stride=stride), :])
        out[pl.ds(c, picked.shape[0], stride=4), :] = product(picked, high) + product(picked, low)


def one_hot(index_row, count):
    rows = lax.broadcasted_iota(jnp.int32, (count, index_row.shape[1]), 0)
    return jnp.where(rows == index_row, 1.0, 0.0).astype(jnp.bfloat16)


def flux_body(
    use_slot,
    slot_row,
    table,
    weights,
    surf_temp,
    surf_hum,
    hum_factor,
    log_mom,
    cell_weight,
    rows_out,
    slot_sums,
    held,
    rows,
    contrib,
    in_sem,
    out_sem,
):
    blocks = held.shape[0]
    parts = blocks // GROUP

    def fetch(p):
        share = pl.ds(pl.multiple_of(p * GROUP, GROUP), GROUP)
        return pltpu.make_async_copy(weights.at[share], held.at[share], in_sem.at[p])

    def put(p):
        share = pl.ds(pl.multiple_of(p * (GROUP * F), GROUP * F), GROUP * F)
        return pltpu.make_async_copy(rows.at[share], rows_out.at[share], out_sem.at[p])

    for p in range(parts):
        fetch(p).start()

    def part(p, _):
        base = p * GROUP
        fetch(p).wait()
        for i in range(0, GROUP, 2):
            k = base + i
            both = lax.dot_general(
                jnp.concatenate([table[use_slot[k]], table[use_slot[k + 1]]], axis=0),
                held[pl.ds(k, 2)].reshape(2 * BLK, ACELL),
                (((1,), (1,)), ((), ())),
                preferred_element_type=jnp.float32,
            )
            rows[pl.ds(pl.multiple_of(k * F, F), F), :] = both[:F, :BLK]
            rows[pl.ds(pl.multiple_of(k * F + F, F), F), :] = both[F:, BLK:]
        mine = pl.ds(pl.multiple_of(base, GROUP), GROUP)
        row = lambda f: pl.ds(base * F + f, GROUP, stride=F)
        fluxes = flux_rows(
            *(rows[row(f), :] for f in range(4)),
            surf_temp[mine, :],
            surf_hum[mine, :],
            hum_factor[mine, :],
            log_mom[mine, :],
        )
        weight = cell_weight[mine, :]
        for f in range(4):
            rows[row(f), :] = weight * fluxes[f]
        put(p).start()
        for i in range(0, GROUP, 2):
            k = base + i
            left = jnp.concatenate(
                [
                    rows[pl.ds(pl.multiple_of(k * F, F), 8), :],
                    rows[pl.ds(pl.multiple_of(k * F + F, F), 8), :],
                ],
                axis=0,
            ).astype(jnp.bfloat16)
            both = product(left, jnp.concatenate([held[k], held[k + 1]], axis=1))
            contrib[pl.ds(pl.multiple_of(k * 8, 8), 8), :] = both[:8, :ACELL]
            contrib[pl.ds(pl.multiple_of(k * 8 + 8, 8), 8), :] = both[8:, ACELL:]
        return 0

    lax.fori_loop(0, parts, part, 0)
    sum_rows(one_hot(slot_row[...], table.shape[0]), contrib, slot_sums, 8)
    for p in range(parts):
        put(p).wait()


def fluxes_of(use_slot, table, weights, cells):
    blocks = weights.shape[0]
    here = pl.BlockSpec(memory_space=VMEM)
    far = pl.BlockSpec(memory_space=pltpu.HBM)
    return pl.pallas_call(
        flux_body,
        out_shape=(
            pltpu.HBM((blocks * F, BLK), jnp.float32),
            jax.ShapeDtypeStruct((table.shape[0] * 4, ACELL), jnp.float32),
        ),
        in_specs=[pl.BlockSpec(memory_space=SMEM), here, here, far] + [here] * 5,
        out_specs=(far, here),
        scratch_shapes=[
            pltpu.VMEM(weights.shape, weights.dtype),
            pltpu.VMEM((blocks * F, BLK), jnp.float32),
            pltpu.VMEM((blocks * 8, ACELL), jnp.float32),
            pltpu.SemaphoreType.DMA((blocks // GROUP,)),
            pltpu.SemaphoreType.DMA((blocks // GROUP,)),
        ],
        compiler_params=pltpu.CompilerParams(vmem_limit_bytes=30 * MIB),
        name="fluxes",
    )(
        use_slot,
        use_slot.reshape(1, -1),
        table,
        pltpu.with_memory_space_constraint(weights, pltpu.HBM),
        *cells,
    )


def ocean_body(ocean_block, rows, hot, passive_weight, ocean_sums, partial):
    step = pl.program_id(0)

    @pl.when(step == 0)
    def _():
        ocean_sums[...] = jnp.zeros_like(ocean_sums)

    is_flux = lax.broadcasted_iota(jnp.int32, (8, BLK), 0) < 4
    for i in range(GROUP):
        factor = passive_weight[i : i + 1, :]
        value = rows[i * F : (i + 1) * F, :]
        value = jnp.concatenate(
            [jnp.where(is_flux, value[:8], value[:8] * factor), value[8:] * factor], axis=0
        )
        both = product(jnp.concatenate(two_parts(value), axis=0), hot[i])
        partial[i * F : (i + 1) * F, :] = both[:F] + both[F:]
    for i in range(GROUP):
        target = ocean_block[step * GROUP + i]
        ocean_sums[target] = ocean_sums[target] + partial[i * F : (i + 1) * F, :]


def ocean_of(ocean_block, rows, hot, passive_weight, owners):
    blocks = hot.shape[0]
    return pl.pallas_call(
        ocean_body,
        out_shape=jax.ShapeDtypeStruct((owners, F, OCELL), jnp.float32),
        grid_spec=pltpu.PrefetchScalarGridSpec(
            num_scalar_prefetch=1,
            grid=(blocks // GROUP,),
            in_specs=[
                pl.BlockSpec((GROUP * F, BLK), lambda s, _: (s, 0)),
                pl.BlockSpec((GROUP, BLK, OCELL), lambda s, _: (s, 0, 0)),
                pl.BlockSpec((GROUP, BLK), lambda s, _: (s, 0)),
            ],
            out_specs=pl.BlockSpec((owners, F, OCELL), lambda s, _: (0, 0, 0)),
            scratch_shapes=[pltpu.VMEM((GROUP * F, OCELL), jnp.float32)],
        ),
        compiler_params=pltpu.CompilerParams(vmem_limit_bytes=16 * MIB),
        cost_estimate=pl.CostEstimate(
            flops=128 * rows.size, bytes_accessed=12 * rows.size, transcendentals=0
        ),
        name="ocean",
    )(
        ocean_block,
        pltpu.with_memory_space_constraint(rows, pltpu.HBM),
        pltpu.with_memory_space_constraint(hot, pltpu.HBM),
        passive_weight,
    )


def owner_body(request_row, returned, out):
    sum_rows(one_hot(request_row[...], out.shape[0] // 4), returned, out, 4)


def owner_sums_of(request_row, returned, local_blocks):
    here = pl.BlockSpec(memory_space=VMEM)
    return pl.pallas_call(
        owner_body,
        out_shape=jax.ShapeDtypeStruct((local_blocks * 4, ACELL), jnp.float32),
        in_specs=[here, here],
        out_specs=here,
        compiler_params=pltpu.CompilerParams(vmem_limit_bytes=8 * MIB),
        name="owner_sums",
    )(request_row, returned)


def sum_over(x, axis):
    ranks = lax.axis_size(axis)
    bit = 1
    while bit < ranks:
        x = x + lax.ppermute(x, axis, [(i, i ^ bit) for i in range(ranks)])
        bit *= 2
    return x


def per_device(
    atm_fields,
    weights,
    surf_temp,
    surf_hum,
    roughness,
    cell_area,
    need_list,
    use_slot,
    ocean_block,
    ocean_cell,
    cell_count,
    ice_mask,
):
    owners = lax.axis_size("atm")
    local_blocks = atm_fields.shape[0]
    requests = lax.all_to_all(need_list[0], "atm", split_axis=0, concat_axis=0, tiled=True)
    table = lax.all_to_all(serve(requests, atm_fields), "atm", split_axis=0, concat_axis=0, tiled=True)
    hot, surf_temp, surf_hum, request_row = prep(ocean_cell, surf_temp, surf_hum, requests)
    ice_frac = ice_mask.astype(jnp.float32)
    is_live = jnp.arange(BLK, dtype=jnp.int32)[None, :] < cell_count[:, None]
    cell_weight = jnp.where(is_live, cell_area, 0.0)
    log_mom = jnp.log(ref_height / roughness)
    cells = (surf_temp, surf_hum, 1.0 - 0.6 * ice_frac, log_mom, cell_weight)
    passive_weight = cell_weight * (1.0 - 0.7 * ice_frac)
    rows, slot_sums = fluxes_of(use_slot, table, weights, cells)
    returned = lax.all_to_all(slot_sums, "atm", split_axis=0, concat_axis=0, tiled=True)
    ocean_sums = ocean_of(ocean_block, rows, hot, passive_weight, owners)
    ocean_parts = lax.all_to_all(ocean_sums, "atm", split_axis=0, concat_axis=0, tiled=True)
    owner_sums = owner_sums_of(request_row, returned, local_blocks)
    atm_flux = sum_over(owner_sums, "ocn").reshape(local_blocks, 4, ACELL)
    ocean_flux = jnp.sum(ocean_parts, axis=0, keepdims=True)
    return (atm_flux, ocean_flux)


def solution(mesh):
    placed = (
        P("atm", None, None),
        P(("ocn", "atm"), None, None),
        P(("ocn", "atm"), None),
        P(("ocn", "atm"), None),
        P(("ocn", "atm"), None),
        P(("ocn", "atm"), None),
        P(("ocn", "atm"), None, None),
        P(("ocn", "atm")),
        P(("ocn", "atm")),
        P(("ocn", "atm"), None),
        P(("ocn", "atm")),
        P(("ocn", "atm"), None),
    )
    return jax.shard_map(
        per_device,
        mesh=mesh,
        in_specs=placed,
        out_specs=(P("atm", None, None), P(("ocn", "atm"), None, None)),
        check_vma=False,
    )
```

```python
import math

import jax
import jax.numpy as jnp
from jax import lax
from jax.experimental import pallas as pl
from jax.experimental.pallas import tpu as pltpu
from jax.sharding import PartitionSpec as P

F = 32
BLK = 128
ACELL = 128
OCELL = 128
CAP = 4
ITERS = 8

ref_height = 10.0
karman = 0.4
buoyancy = 0.5
flux_scale = 40.0

GROUP = 64
SLOT_ROWS = CAP * 4
OWNER_ROWS = SLOT_ROWS + F
MIB = 1 << 20
VMEM = pltpu.VMEM
SMEM = pltpu.SMEM

ARCTAN = (
    0.9999999952,
    -0.3333319239,
    0.1999324926,
    -0.1416585733,
    0.1012280370,
    -0.0507783010,
)


def arctan_half(t):
    z = t * t
    total = jnp.full_like(z, ARCTAN[-1])
    for c in ARCTAN[-2::-1]:
        total = total * z + c
    return total * t


def flux_rows(mapped_u, mapped_v, mapped_t, mapped_q, surf_temp, surf_hum, hum_factor, log_mom):
    wind_u = 6.0 * mapped_u
    wind_v = 6.0 * mapped_v
    square_speed = wind_u * wind_u + wind_v * wind_v + 1.0
    wind_speed = jnp.sqrt(square_speed)
    temp_diff = mapped_t - surf_temp
    hum_diff = (mapped_q - surf_hum) * hum_factor
    log_heat = log_mom + math.log(10.0)
    gain = (ref_height * buoyancy) * (temp_diff + 0.2 * hum_diff) / square_speed
    from_mom = log_mom
    from_heat = log_heat
    for sweep in range(ITERS):
        stability = jnp.clip(gain * from_mom * from_mom / from_heat, -5.0, 1.0)
        unstable = jnp.minimum(stability, 0.0)
        square = jnp.sqrt(1.0 - 16.0 * unstable)
        root = jnp.sqrt(square)
        half_square = 0.5 + 0.5 * square
        half_root = 0.5 + 0.5 * root
        log_square = jnp.log(half_square)
        log_both = jnp.log(half_root * half_root * half_square)
        turn = arctan_half((root - 1.0) / (root + 1.0))
        stable = stability >= 0.0
        psi_stable = -5.0 * stability
        psi_mom = jnp.where(stable, psi_stable, log_both - 2.0 * turn)
        psi_heat = jnp.where(stable, psi_stable, 2.0 * log_square)
        from_mom = log_mom - psi_mom
        from_heat = log_heat - psi_heat
    fric_vel = karman * wind_speed / from_mom
    drag = flux_scale * fric_vel * fric_vel / wind_speed
    carry = -flux_scale * karman * fric_vel / from_heat
    return drag * wind_u, drag * wind_v, carry * temp_diff, carry * hum_diff


def serve_body(requests, fields, out):
    def owner(d, _):
        for c in range(CAP):
            out[d * CAP + c] = fields[requests[d, c]]
        return 0

    lax.fori_loop(0, out.shape[0] // CAP, owner, 0)


def serve(requests, fields):
    return pl.pallas_call(
        serve_body,
        out_shape=jax.ShapeDtypeStruct((requests.size,) + fields.shape[1:], fields.dtype),
        in_specs=[pl.BlockSpec(memory_space=SMEM), pl.BlockSpec(memory_space=VMEM)],
        out_specs=pl.BlockSpec(memory_space=VMEM),
        compiler_params=pltpu.CompilerParams(vmem_limit_bytes=8 * MIB),
        name="serve",
    )(requests, fields)


def prep_body(ocean_cell, surf_temp, surf_hum, requests, hot, temp, hum, request_row):
    request_row[...] = requests[...]
    temp[...] = surf_temp[...]
    hum[...] = surf_hum[...]
    target = lax.broadcasted_iota(jnp.int32, (OCELL, BLK), 0)
    for i in range(hot.shape[0]):
        hot[i] = jnp.where(target == ocean_cell[i : i + 1, :], 1.0, 0.0).astype(jnp.bfloat16).T


def prep(ocean_cell, surf_temp, surf_hum, requests):
    blocks = ocean_cell.shape[0]
    part = pl.BlockSpec((GROUP, BLK), lambda s: (s, 0))
    flat = jax.ShapeDtypeStruct((blocks, BLK), jnp.float32)
    line = pl.BlockSpec((1, requests.size), lambda s: (0, 0))
    return pl.pallas_call(
        prep_body,
        out_shape=(pltpu.HBM((blocks, BLK, OCELL), jnp.bfloat16), flat, flat, jax.ShapeDtypeStruct((1, requests.size), jnp.int32)),
        grid=(blocks // GROUP,),
        in_specs=[part] * 3 + [line],
        out_specs=(pl.BlockSpec((GROUP, BLK, OCELL), lambda s: (s, 0, 0)), part, part, line),
        compiler_params=pltpu.CompilerParams(vmem_limit_bytes=16 * MIB),
        cost_estimate=pl.CostEstimate(
            flops=2 * blocks * BLK * OCELL,
            bytes_accessed=2 * blocks * BLK * OCELL,
            transcendentals=0,
        ),
        name="prep",
    )(ocean_cell, surf_temp, surf_hum, requests.T.reshape(1, -1))


def two_parts(value):
    high = value.astype(jnp.bfloat16)
    return high, (value - high.astype(jnp.float32)).astype(jnp.bfloat16)


def product(left, right):
    return jnp.dot(left, right, preferred_element_type=jnp.float32)


def one_hot(of_row, index_row):
    return jnp.where(of_row == index_row, 1.0, 0.0).astype(jnp.bfloat16)


def picked_sum(picked, values):
    high, low = two_parts(values)
    return product(picked, high) + product(picked, low)


def couple_body(
    use_slot,
    ocean_block,
    slot_row,
    table,
    weights,
    hot_far,
    surf_temp,
    surf_hum,
    hum_factor,
    log_mom,
    cell_weight,
    passive_weight,
    out,
    held,
    hot,
    rows_even,
    rows_odd,
    partial,
    contrib,
    sem,
):
    blocks = held.shape[0]
    parts = blocks // GROUP
    owners = out.shape[0] // OWNER_ROWS

    def fetch(p):
        share = pl.ds(pl.multiple_of(p * GROUP, GROUP), GROUP)
        return (
            pltpu.make_async_copy(weights.at[share], held.at[share], sem.at[p]),
            pltpu.make_async_copy(hot_far.at[share], hot.at[share], sem.at[parts + p]),
        )

    for p in range(parts):
        for copy in fetch(p):
            copy.start()
    out[...] = jnp.zeros_like(out)
    is_flux = lax.broadcasted_iota(jnp.int32, (8, BLK), 0) < 4

    def map_part(p, rows):
        base = p * GROUP
        for i in range(0, GROUP, 2):
            k = base + i
            both = lax.dot_general(
                jnp.concatenate([table[use_slot[0, k]], table[use_slot[0, k + 1]]], axis=0),
                held[pl.ds(k, 2)].reshape(2 * BLK, ACELL),
                (((1,), (1,)), ((), ())),
                preferred_element_type=jnp.float32,
            )
            rows[i * F : (i + 1) * F, :] = both[:F, :BLK]
            rows[(i + 1) * F : (i + 2) * F, :] = both[F:, BLK:]

    def flux_part(p, rows):
        mine = pl.ds(pl.multiple_of(p * GROUP, GROUP), GROUP)
        fluxes = flux_rows(
            *(rows[pl.ds(f, GROUP, stride=F), :] for f in range(4)),
            surf_temp[mine, :],
            surf_hum[mine, :],
            hum_factor[mine, :],
            log_mom[mine, :],
        )
        weight = cell_weight[mine, :]
        for f in range(4):
            rows[pl.ds(f, GROUP, stride=F), :] = weight * fluxes[f]

    def sum_part(p, rows):
        base = p * GROUP
        for i in range(0, GROUP, 2):
            k = base + i
            left = jnp.concatenate(
                [rows[i * F : i * F + 8, :], rows[(i + 1) * F : (i + 1) * F + 8, :]], axis=0
            ).astype(jnp.bfloat16)
            both = product(left, jnp.concatenate([held[k], held[k + 1]], axis=1))
            contrib[pl.ds(pl.multiple_of(k * 8, 8), 8), :] = both[:8, :ACELL]
            contrib[pl.ds(pl.multiple_of(k * 8 + 8, 8), 8), :] = both[8:, ACELL:]
        for i in range(GROUP):
            k = base + i
            factor = passive_weight[pl.ds(k, 1), :]
            value = rows[i * F : (i + 1) * F, :]
            value = jnp.concatenate(
                [jnp.where(is_flux, value[:8], value[:8] * factor), value[8:] * factor], axis=0
            )
            both = product(jnp.concatenate(two_parts(value), axis=0), hot[k])
            partial[i * F : (i + 1) * F, :] = both[:F] + both[F:]
        for i in range(GROUP):
            target = pl.ds(
                pl.multiple_of(ocean_block[0, base + i] * OWNER_ROWS + SLOT_ROWS, SLOT_ROWS), F
            )
            out[target, :] = out[target, :] + partial[i * F : (i + 1) * F, :]

    def arrive(p, which):
        fetch(p)[which].wait()

    def step(p, _):
        arrive(p, 0)
        map_part(p, rows_even)
        flux_part(p, rows_even)
        arrive(p, 1)
        sum_part(p, rows_even)
        return 0

    lax.fori_loop(0, parts, step, 0)

    order = lax.broadcasted_iota(jnp.int32, (owners * CAP, blocks), 0)
    slot_of = lax.rem(order, owners) * CAP + order // owners
    picked = one_hot(slot_of, slot_row[...])
    for c in range(4):
        sums = picked_sum(picked, contrib[pl.ds(c, blocks, stride=8), :])
        for column in range(CAP):
            out[pl.ds(column * 4 + c, owners, stride=OWNER_ROWS), :] = sums[
                column * owners : (column + 1) * owners
            ]


def couple(slot_row, block_row, table, weights, hot, cells, owners):
    blocks = weights.shape[0]
    here = pl.BlockSpec(memory_space=VMEM)
    far = pl.BlockSpec(memory_space=pltpu.HBM)
    line = pl.BlockSpec(memory_space=SMEM)
    return pl.pallas_call(
        couple_body,
        out_shape=jax.ShapeDtypeStruct((owners * OWNER_ROWS, ACELL), jnp.float32),
        in_specs=[line, line, here, here, far, far] + [here] * 6,
        out_specs=here,
        scratch_shapes=[
            pltpu.VMEM(weights.shape, weights.dtype),
            pltpu.VMEM(hot.shape, hot.dtype),
            pltpu.VMEM((GROUP * F, BLK), jnp.float32),
            pltpu.VMEM((GROUP * F, BLK), jnp.float32),
            pltpu.VMEM((GROUP * F, OCELL), jnp.float32),
            pltpu.VMEM((blocks * 8, ACELL), jnp.float32),
            pltpu.SemaphoreType.DMA((2 * (blocks // GROUP),)),
        ],
        compiler_params=pltpu.CompilerParams(vmem_limit_bytes=44 * MIB),
        name="couple",
    )(
        slot_row,
        block_row,
        slot_row,
        table,
        pltpu.with_memory_space_constraint(weights, pltpu.HBM),
        pltpu.with_memory_space_constraint(hot, pltpu.HBM),
        *cells,
    )


def owner_body(request_row, returned, owner_sums, ocean_flux):
    sources = returned.shape[0] // OWNER_ROWS
    shape = (owner_sums.shape[0] // 4, request_row.shape[1])
    picked = one_hot(lax.broadcasted_iota(jnp.int32, shape, 0), request_row[...])
    for c in range(4):
        values = jnp.concatenate(
            [
                returned[pl.ds(column * 4 + c, sources, stride=OWNER_ROWS), :]
                for column in range(CAP)
            ],
            axis=0,
        )
        owner_sums[pl.ds(c, shape[0], stride=4), :] = picked_sum(picked, values)
    total = returned[SLOT_ROWS:OWNER_ROWS, :]
    for source in range(1, sources):
        first = source * OWNER_ROWS
        total = total + returned[first + SLOT_ROWS : first + OWNER_ROWS, :]
    ocean_flux[0] = total


def owner_sums_of(request_row, returned, local_blocks):
    here = pl.BlockSpec(memory_space=VMEM)
    return pl.pallas_call(
        owner_body,
        out_shape=(
            jax.ShapeDtypeStruct((local_blocks * 4, ACELL), jnp.float32),
            jax.ShapeDtypeStruct((1, F, OCELL), jnp.float32),
        ),
        in_specs=[here, here],
        out_specs=(here, here),
        compiler_params=pltpu.CompilerParams(vmem_limit_bytes=8 * MIB),
        name="owner_sums",
    )(request_row, returned)


def sum_over(x, axis):
    ranks = lax.axis_size(axis)
    bit = 1
    while bit < ranks:
        mask = ranks - 1 if 2 * bit == ranks else bit
        x = x + lax.ppermute(x, axis, [(i, i ^ mask) for i in range(ranks)])
        bit *= 2
    return x


def per_device(
    atm_fields,
    weights,
    surf_temp,
    surf_hum,
    roughness,
    cell_area,
    need_list,
    use_slot,
    ocean_block,
    ocean_cell,
    cell_count,
    ice_mask,
):
    owners = lax.axis_size("atm")
    local_blocks = atm_fields.shape[0]
    requests = lax.all_to_all(need_list[0], "atm", split_axis=0, concat_axis=0, tiled=True)
    table = lax.all_to_all(serve(requests, atm_fields), "atm", split_axis=0, concat_axis=0, tiled=True)
    hot, surf_temp, surf_hum, request_row = prep(ocean_cell, surf_temp, surf_hum, requests)
    ice_frac = ice_mask.astype(jnp.float32)
    is_live = jnp.arange(BLK, dtype=jnp.int32)[None, :] < cell_count[:, None]
    cell_weight = jnp.where(is_live, cell_area, 0.0)
    log_mom = jnp.log(ref_height / roughness)
    passive_weight = cell_weight * (1.0 - 0.7 * ice_frac)
    cells = (surf_temp, surf_hum, 1.0 - 0.6 * ice_frac, log_mom, cell_weight, passive_weight)
    lines = (use_slot.reshape(1, -1), ocean_block.reshape(1, -1))
    sums = couple(*lines, table, weights, hot, cells, owners)
    returned = lax.all_to_all(sums, "atm", split_axis=0, concat_axis=0, tiled=True)
    owner_sums, ocean_flux = owner_sums_of(request_row, returned, local_blocks)
    atm_flux = sum_over(owner_sums, "ocn").reshape(local_blocks, 4, ACELL)
    return (atm_flux, ocean_flux)


def solution(mesh):
    placed = (
        P("atm", None, None),
        P(("ocn", "atm"), None, None),
        P(("ocn", "atm"), None),
        P(("ocn", "atm"), None),
        P(("ocn", "atm"), None),
        P(("ocn", "atm"), None),
        P(("ocn", "atm"), None, None),
        P(("ocn", "atm")),
        P(("ocn", "atm")),
        P(("ocn", "atm"), None),
        P(("ocn", "atm")),
        P(("ocn", "atm"), None),
    )
    return jax.shard_map(
        per_device,
        mesh=mesh,
        in_specs=placed,
        out_specs=(P("atm", None, None), P(("ocn", "atm"), None, None)),
        check_vma=False,
    )
```

```python
import math

import jax
import jax.numpy as jnp
from jax import lax
from jax.experimental import pallas as pl
from jax.experimental.pallas import tpu as pltpu
from jax.sharding import PartitionSpec as P

F = 32
BLK = 128
ACELL = 128
OCELL = 128
CAP = 4
ITERS = 8

ref_height = 10.0
karman = 0.4
buoyancy = 0.5
flux_scale = 40.0

GROUP = 64
MIB = 1 << 20
ADD_COST = pl.CostEstimate(flops=1500000000, bytes_accessed=3 << 17, transcendentals=0)
VMEM = pltpu.VMEM
SMEM = pltpu.SMEM

ARCTAN = (
    0.9999999952,
    -0.3333319239,
    0.1999324926,
    -0.1416585733,
    0.1012280370,
    -0.0507783010,
)


def arctan_half(t):
    z = t * t
    total = jnp.full_like(z, ARCTAN[-1])
    for c in ARCTAN[-2::-1]:
        total = total * z + c
    return total * t


def flux_rows(mapped_u, mapped_v, mapped_t, mapped_q, surf_temp, surf_hum, hum_factor, log_mom):
    wind_u = 6.0 * mapped_u
    wind_v = 6.0 * mapped_v
    square_speed = wind_u * wind_u + wind_v * wind_v + 1.0
    wind_speed = jnp.sqrt(square_speed)
    temp_diff = mapped_t - surf_temp
    hum_diff = (mapped_q - surf_hum) * hum_factor
    log_heat = log_mom + math.log(10.0)
    gain = (ref_height * buoyancy) * (temp_diff + 0.2 * hum_diff) / square_speed
    from_mom = log_mom
    from_heat = log_heat
    for sweep in range(ITERS):
        stability = jnp.clip(gain * from_mom * from_mom / from_heat, -5.0, 1.0)
        unstable = jnp.minimum(stability, 0.0)
        square = jnp.sqrt(1.0 - 16.0 * unstable)
        root = jnp.sqrt(square)
        half_square = 0.5 + 0.5 * square
        half_root = 0.5 + 0.5 * root
        log_square = jnp.log(half_square)
        log_both = jnp.log(half_root * half_root * half_square)
        turn = arctan_half((root - 1.0) / (root + 1.0))
        stable = stability >= 0.0
        psi_stable = -5.0 * stability
        psi_mom = jnp.where(stable, psi_stable, log_both - 2.0 * turn)
        psi_heat = jnp.where(stable, psi_stable, 2.0 * log_square)
        from_mom = log_mom - psi_mom
        from_heat = log_heat - psi_heat
    fric_vel = karman * wind_speed / from_mom
    drag = flux_scale * fric_vel * fric_vel / wind_speed
    carry = -flux_scale * karman * fric_vel / from_heat
    return drag * wind_u, drag * wind_v, carry * temp_diff, carry * hum_diff


def serve_body(requests, fields, out):
    def owner(d, _):
        for c in range(CAP):
            out[d * CAP + c] = fields[requests[d, c]]
        return 0

    lax.fori_loop(0, out.shape[0] // CAP, owner, 0)


def serve(requests, fields):
    return pl.pallas_call(
        serve_body,
        out_shape=jax.ShapeDtypeStruct((requests.size,) + fields.shape[1:], fields.dtype),
        in_specs=[pl.BlockSpec(memory_space=SMEM), pl.BlockSpec(memory_space=VMEM)],
        out_specs=pl.BlockSpec(memory_space=VMEM),
        compiler_params=pltpu.CompilerParams(vmem_limit_bytes=8 * MIB),
        name="serve",
    )(requests, fields)


def prep_body(ocean_cell, surf_temp, surf_hum, requests, hot, temp, hum, request_row):
    request_row[...] = requests[...]
    temp[...] = surf_temp[...]
    hum[...] = surf_hum[...]
    target = lax.broadcasted_iota(jnp.int32, (OCELL, BLK), 0)
    for i in range(hot.shape[0]):
        hot[i] = jnp.where(target == ocean_cell[i : i + 1, :], 1.0, 0.0).astype(jnp.bfloat16).T


def prep(ocean_cell, surf_temp, surf_hum, requests):
    blocks = ocean_cell.shape[0]
    part = pl.BlockSpec((GROUP, BLK), lambda s: (s, 0))
    flat = jax.ShapeDtypeStruct((blocks, BLK), jnp.float32)
    line = pl.BlockSpec((1, requests.size), lambda s: (0, 0))
    return pl.pallas_call(
        prep_body,
        out_shape=(pltpu.HBM((blocks, BLK, OCELL), jnp.bfloat16), flat, flat, jax.ShapeDtypeStruct((1, requests.size), jnp.int32)),
        grid=(blocks // GROUP,),
        in_specs=[part] * 3 + [line],
        out_specs=(pl.BlockSpec((GROUP, BLK, OCELL), lambda s: (s, 0, 0)), part, part, line),
        compiler_params=pltpu.CompilerParams(vmem_limit_bytes=16 * MIB),
        cost_estimate=pl.CostEstimate(
            flops=2 * blocks * BLK * OCELL,
            bytes_accessed=2 * blocks * BLK * OCELL,
            transcendentals=0,
        ),
        name="prep",
    )(ocean_cell, surf_temp, surf_hum, requests.reshape(1, -1))


def two_parts(value):
    high = value.astype(jnp.bfloat16)
    return high, (value - high.astype(jnp.float32)).astype(jnp.bfloat16)


def product(left, right):
    return jnp.dot(left, right, preferred_element_type=jnp.float32)


def sum_rows(picked, values, out, stride):
    entries = picked.shape[1]
    for c in range(4):
        high, low = two_parts(values[pl.ds(c, entries, stride=stride), :])
        out[pl.ds(c, picked.shape[0], stride=4), :] = product(picked, high) + product(picked, low)


def one_hot(index_row, count):
    rows = lax.broadcasted_iota(jnp.int32, (count, index_row.shape[1]), 0)
    return jnp.where(rows == index_row, 1.0, 0.0).astype(jnp.bfloat16)


def flux_body(
    use_slot,
    slot_row,
    table,
    weights,
    surf_temp,
    surf_hum,
    hum_factor,
    log_mom,
    cell_weight,
    rows_out,
    slot_sums,
    held,
    rows,
    contrib,
    in_sem,
    out_sem,
):
    blocks = held.shape[0]
    parts = blocks // GROUP

    def fetch(p):
        share = pl.ds(pl.multiple_of(p * GROUP, GROUP), GROUP)
        return pltpu.make_async_copy(weights.at[share], held.at[share], in_sem.at[p])

    def put(p):
        share = pl.ds(pl.multiple_of(p * (GROUP * F), GROUP * F), GROUP * F)
        return pltpu.make_async_copy(rows.at[share], rows_out.at[share], out_sem.at[p])

    for p in range(parts):
        fetch(p).start()

    def part(p, _):
        base = p * GROUP
        fetch(p).wait()
        for i in range(0, GROUP, 2):
            k = base + i
            both = lax.dot_general(
                jnp.concatenate([table[use_slot[0, k]], table[use_slot[0, k + 1]]], axis=0),
                held[pl.ds(k, 2)].reshape(2 * BLK, ACELL),
                (((1,), (1,)), ((), ())),
                preferred_element_type=jnp.float32,
            )
            rows[pl.ds(pl.multiple_of(k * F, F), F), :] = both[:F, :BLK]
            rows[pl.ds(pl.multiple_of(k * F + F, F), F), :] = both[F:, BLK:]
        mine = pl.ds(pl.multiple_of(base, GROUP), GROUP)
        row = lambda f: pl.ds(base * F + f, GROUP, stride=F)
        fluxes = flux_rows(
            *(rows[row(f), :] for f in range(4)),
            surf_temp[mine, :],
            surf_hum[mine, :],
            hum_factor[mine, :],
            log_mom[mine, :],
        )
        weight = cell_weight[mine, :]
        for f in range(4):
            rows[row(f), :] = weight * fluxes[f]
        put(p).start()
        for i in range(0, GROUP, 2):
            k = base + i
            left = jnp.concatenate(
                [
                    rows[pl.ds(pl.multiple_of(k * F, F), 8), :],
                    rows[pl.ds(pl.multiple_of(k * F + F, F), 8), :],
                ],
                axis=0,
            ).astype(jnp.bfloat16)
            both = product(left, jnp.concatenate([held[k], held[k + 1]], axis=1))
            contrib[pl.ds(pl.multiple_of(k * 8, 8), 8), :] = both[:8, :ACELL]
            contrib[pl.ds(pl.multiple_of(k * 8 + 8, 8), 8), :] = both[8:, ACELL:]
        return 0

    lax.fori_loop(0, parts, part, 0)
    sum_rows(one_hot(slot_row[...], table.shape[0]), contrib, slot_sums, 8)
    for p in range(parts):
        put(p).wait()


def fluxes_of(slot_row, table, weights, cells):
    blocks = weights.shape[0]
    here = pl.BlockSpec(memory_space=VMEM)
    far = pl.BlockSpec(memory_space=pltpu.HBM)
    return pl.pallas_call(
        flux_body,
        out_shape=(
            pltpu.HBM((blocks * F, BLK), jnp.float32),
            jax.ShapeDtypeStruct((table.shape[0] * 4, ACELL), jnp.float32),
        ),
        in_specs=[pl.BlockSpec(memory_space=SMEM), here, here, far] + [here] * 5,
        out_specs=(far, here),
        scratch_shapes=[
            pltpu.VMEM(weights.shape, weights.dtype),
            pltpu.VMEM((blocks * F, BLK), jnp.float32),
            pltpu.VMEM((blocks * 8, ACELL), jnp.float32),
            pltpu.SemaphoreType.DMA((blocks // GROUP,)),
            pltpu.SemaphoreType.DMA((blocks // GROUP,)),
        ],
        compiler_params=pltpu.CompilerParams(vmem_limit_bytes=30 * MIB),
        name="fluxes",
    )(
        slot_row,
        slot_row,
        table,
        pltpu.with_memory_space_constraint(weights, pltpu.HBM),
        *cells,
    )


def ocean_body(ocean_block, rows_far, hot_far, passive_weight, ocean_sums, rows, hot, partial, sem):
    parts = hot.shape[0] // GROUP

    def fetch(p):
        flat = pl.ds(pl.multiple_of(p * (GROUP * F), GROUP * F), GROUP * F)
        share = pl.ds(pl.multiple_of(p * GROUP, GROUP), GROUP)
        return (
            pltpu.make_async_copy(rows_far.at[flat], rows.at[flat], sem.at[p]),
            pltpu.make_async_copy(hot_far.at[share], hot.at[share], sem.at[parts + p]),
        )

    for p in range(parts):
        for copy in fetch(p):
            copy.start()
    ocean_sums[...] = jnp.zeros_like(ocean_sums)
    is_flux = lax.broadcasted_iota(jnp.int32, (8, BLK), 0) < 4

    def part(p, _):
        for copy in fetch(p):
            copy.wait()
        for i in range(GROUP):
            k = p * GROUP + i
            factor = passive_weight[pl.ds(k, 1), :]
            value = rows[pl.ds(pl.multiple_of(k * F, F), F), :]
            value = jnp.concatenate(
                [jnp.where(is_flux, value[:8], value[:8] * factor), value[8:] * factor], axis=0
            )
            both = product(jnp.concatenate(two_parts(value), axis=0), hot[k])
            partial[i * F : (i + 1) * F, :] = both[:F] + both[F:]
        for i in range(GROUP):
            target = ocean_block[0, p * GROUP + i]
            ocean_sums[target] = ocean_sums[target] + partial[i * F : (i + 1) * F, :]
        return 0

    lax.fori_loop(0, parts, part, 0)


def ocean_of(block_row, rows, hot, passive_weight, owners):
    here = pl.BlockSpec(memory_space=VMEM)
    far = pl.BlockSpec(memory_space=pltpu.HBM)
    return pl.pallas_call(
        ocean_body,
        out_shape=jax.ShapeDtypeStruct((owners, F, OCELL), jnp.float32),
        in_specs=[pl.BlockSpec(memory_space=SMEM), far, far, here],
        out_specs=here,
        scratch_shapes=[
            pltpu.VMEM(rows.shape, rows.dtype),
            pltpu.VMEM(hot.shape, hot.dtype),
            pltpu.VMEM((GROUP * F, OCELL), jnp.float32),
            pltpu.SemaphoreType.DMA((2 * (hot.shape[0] // GROUP),)),
        ],
        compiler_params=pltpu.CompilerParams(vmem_limit_bytes=28 * MIB),
        cost_estimate=pl.CostEstimate(
            flops=128 * rows.size, bytes_accessed=12 * rows.size, transcendentals=0
        ),
        name="ocean",
    )(
        block_row,
        pltpu.with_memory_space_constraint(rows, pltpu.HBM),
        pltpu.with_memory_space_constraint(hot, pltpu.HBM),
        passive_weight,
    )


def owner_body(request_row, returned, ocean_sums, out):
    sum_rows(one_hot(request_row[...], out.shape[0] // 4), returned, out, 4)


def owner_sums_of(request_row, returned, ocean_sums, local_blocks):
    here = pl.BlockSpec(memory_space=VMEM)
    return pl.pallas_call(
        owner_body,
        out_shape=jax.ShapeDtypeStruct((local_blocks * 4, ACELL), jnp.float32),
        in_specs=[here, here, pl.BlockSpec(memory_space=pl.ANY)],
        out_specs=here,
        compiler_params=pltpu.CompilerParams(vmem_limit_bytes=8 * MIB),
        name="owner_sums",
    )(request_row, returned, ocean_sums)


def add_body(left, right, out):
    out[...] = left[...] + right[...]


def add(left, right):
    here = pl.BlockSpec(memory_space=VMEM)
    return pl.pallas_call(
        add_body,
        out_shape=jax.ShapeDtypeStruct(left.shape, left.dtype),
        in_specs=[here, here],
        out_specs=here,
        compiler_params=pltpu.CompilerParams(vmem_limit_bytes=8 * MIB),
        cost_estimate=ADD_COST,
        name="add",
    )(left, right)


def sum_over_ring(x, axis, other):
    ranks, places = lax.axis_size(axis), lax.axis_size(other)
    bit = 1
    while bit < ranks:
        mask = ranks - 1 if 2 * bit == ranks else bit

        def partner(i, turn):
            return (((i - turn) % ranks) ^ mask) + turn

        pairs = [
            (i * places + p, partner(i, (p % 2) * (ranks // 4)) % ranks * places + p)
            for i in range(ranks)
            for p in range(places)
        ]
        x = add(x, lax.ppermute(x, (axis, other), pairs))
        bit *= 2
    return x


def per_device(
    atm_fields,
    weights,
    surf_temp,
    surf_hum,
    roughness,
    cell_area,
    need_list,
    use_slot,
    ocean_block,
    ocean_cell,
    cell_count,
    ice_mask,
):
    owners = lax.axis_size("atm")
    local_blocks = atm_fields.shape[0]
    requests = lax.all_to_all(need_list[0], "atm", split_axis=0, concat_axis=0, tiled=True)
    table = lax.all_to_all(serve(requests, atm_fields), "atm", split_axis=0, concat_axis=0, tiled=True)
    hot, surf_temp, surf_hum, request_row = prep(ocean_cell, surf_temp, surf_hum, requests)
    ice_frac = ice_mask.astype(jnp.float32)
    is_live = jnp.arange(BLK, dtype=jnp.int32)[None, :] < cell_count[:, None]
    cell_weight = jnp.where(is_live, cell_area, 0.0)
    log_mom = jnp.log(ref_height / roughness)
    cells = (surf_temp, surf_hum, 1.0 - 0.6 * ice_frac, log_mom, cell_weight)
    passive_weight = cell_weight * (1.0 - 0.7 * ice_frac)
    rows, slot_sums = fluxes_of(use_slot.reshape(1, -1), table, weights, cells)
    returned = lax.all_to_all(slot_sums, "atm", split_axis=0, concat_axis=0, tiled=True)
    ocean_sums = ocean_of(ocean_block.reshape(1, -1), rows, hot, passive_weight, owners)
    owner_sums = owner_sums_of(request_row, returned, ocean_sums, local_blocks)
    ocean_parts = lax.all_to_all(ocean_sums, "atm", split_axis=0, concat_axis=0, tiled=True)
    atm_flux = sum_over_ring(owner_sums, "ocn", "atm").reshape(local_blocks, 4, ACELL)
    ocean_flux = jnp.sum(ocean_parts, axis=0, keepdims=True)
    return (atm_flux, ocean_flux)


def solution(mesh):
    placed = (
        P("atm", None, None),
        P(("ocn", "atm"), None, None),
        P(("ocn", "atm"), None),
        P(("ocn", "atm"), None),
        P(("ocn", "atm"), None),
        P(("ocn", "atm"), None),
        P(("ocn", "atm"), None, None),
        P(("ocn", "atm")),
        P(("ocn", "atm")),
        P(("ocn", "atm"), None),
        P(("ocn", "atm")),
        P(("ocn", "atm"), None),
    )
    return jax.shard_map(
        per_device,
        mesh=mesh,
        in_specs=placed,
        out_specs=(P("atm", None, None), P(("ocn", "atm"), None, None)),
        check_vma=False,
    )
```

```python
import math

import jax
import jax.numpy as jnp
from jax import lax
from jax.experimental import pallas as pl
from jax.experimental.pallas import tpu as pltpu
from jax.sharding import PartitionSpec as P

F = 32
BLK = 128
ACELL = 128
OCELL = 128
CAP = 4
ITERS = 8

ref_height = 10.0
karman = 0.4
buoyancy = 0.5
flux_scale = 40.0

GROUP = 64
FLUX_GROUP = 96
MIB = 1 << 20
ADD_COST = pl.CostEstimate(flops=4000000000, bytes_accessed=3 << 17, transcendentals=0)
VMEM = pltpu.VMEM
SMEM = pltpu.SMEM

ARCTAN = (
    0.9999999952,
    -0.3333319239,
    0.1999324926,
    -0.1416585733,
    0.1012280370,
    -0.0507783010,
)


def arctan_half(t):
    z = t * t
    total = jnp.full_like(z, ARCTAN[-1])
    for c in ARCTAN[-2::-1]:
        total = total * z + c
    return total * t


def flux_rows(mapped_u, mapped_v, mapped_t, mapped_q, surf_temp, surf_hum, hum_factor, log_mom):
    wind_u = 6.0 * mapped_u
    wind_v = 6.0 * mapped_v
    square_speed = wind_u * wind_u + wind_v * wind_v + 1.0
    wind_speed = jnp.sqrt(square_speed)
    temp_diff = mapped_t - surf_temp
    hum_diff = (mapped_q - surf_hum) * hum_factor
    log_heat = log_mom + math.log(10.0)
    gain = (ref_height * buoyancy) * (temp_diff + 0.2 * hum_diff) / square_speed
    from_mom = log_mom
    from_heat = log_heat
    for sweep in range(ITERS):
        stability = jnp.clip(gain * from_mom * from_mom / from_heat, -5.0, 1.0)
        unstable = jnp.minimum(stability, 0.0)
        square = jnp.sqrt(1.0 - 16.0 * unstable)
        root = jnp.sqrt(square)
        half_square = 0.5 + 0.5 * square
        half_root = 0.5 + 0.5 * root
        log_square = jnp.log(half_square)
        log_both = jnp.log(half_root * half_root * half_square)
        turn = arctan_half((root - 1.0) / (root + 1.0))
        stable = stability >= 0.0
        psi_stable = -5.0 * stability
        psi_mom = jnp.where(stable, psi_stable, log_both - 2.0 * turn)
        psi_heat = jnp.where(stable, psi_stable, 2.0 * log_square)
        from_mom = log_mom - psi_mom
        from_heat = log_heat - psi_heat
    fric_vel = karman * wind_speed / from_mom
    drag = flux_scale * fric_vel * fric_vel / wind_speed
    carry = -flux_scale * karman * fric_vel / from_heat
    return drag * wind_u, drag * wind_v, carry * temp_diff, carry * hum_diff


def serve_body(requests, fields, out):
    def owner(d, _):
        for c in range(CAP):
            out[d * CAP + c] = fields[requests[d, c]]
        return 0

    lax.fori_loop(0, out.shape[0] // CAP, owner, 0)


def serve(requests, fields):
    return pl.pallas_call(
        serve_body,
        out_shape=jax.ShapeDtypeStruct((requests.size,) + fields.shape[1:], fields.dtype),
        in_specs=[pl.BlockSpec(memory_space=SMEM), pl.BlockSpec(memory_space=VMEM)],
        out_specs=pl.BlockSpec(memory_space=VMEM),
        compiler_params=pltpu.CompilerParams(vmem_limit_bytes=8 * MIB),
        name="serve",
    )(requests, fields)


def prep_body(ocean_cell, surf_temp, surf_hum, requests, hot, temp, hum, request_row):
    request_row[...] = requests[...]
    temp[...] = surf_temp[...]
    hum[...] = surf_hum[...]
    target = lax.broadcasted_iota(jnp.int32, (OCELL, BLK), 0)
    for i in range(hot.shape[0]):
        hot[i] = jnp.where(target == ocean_cell[i : i + 1, :], 1.0, 0.0).astype(jnp.bfloat16).T


def prep(ocean_cell, surf_temp, surf_hum, requests):
    blocks = ocean_cell.shape[0]
    part = pl.BlockSpec((GROUP, BLK), lambda s: (s, 0))
    flat = jax.ShapeDtypeStruct((blocks, BLK), jnp.float32)
    line = pl.BlockSpec((1, requests.size), lambda s: (0, 0))
    return pl.pallas_call(
        prep_body,
        out_shape=(pltpu.HBM((blocks, BLK, OCELL), jnp.bfloat16), flat, flat, jax.ShapeDtypeStruct((1, requests.size), jnp.int32)),
        grid=(blocks // GROUP,),
        in_specs=[part] * 3 + [line],
        out_specs=(pl.BlockSpec((GROUP, BLK, OCELL), lambda s: (s, 0, 0)), part, part, line),
        compiler_params=pltpu.CompilerParams(vmem_limit_bytes=16 * MIB),
        cost_estimate=pl.CostEstimate(
            flops=2 * blocks * BLK * OCELL,
            bytes_accessed=2 * blocks * BLK * OCELL,
            transcendentals=0,
        ),
        name="prep",
    )(ocean_cell, surf_temp, surf_hum, requests.reshape(1, -1))


def two_parts(value):
    high = value.astype(jnp.bfloat16)
    return high, (value - high.astype(jnp.float32)).astype(jnp.bfloat16)


def product(left, right):
    return jnp.dot(left, right, preferred_element_type=jnp.float32)


def sum_rows(picked, values, out, stride):
    entries = picked.shape[1]
    for c in range(4):
        high, low = two_parts(values[pl.ds(c, entries, stride=stride), :])
        out[pl.ds(c, picked.shape[0], stride=4), :] = product(picked, high) + product(picked, low)


def one_hot(index_row, count):
    rows = lax.broadcasted_iota(jnp.int32, (count, index_row.shape[1]), 0)
    return jnp.where(rows == index_row, 1.0, 0.0).astype(jnp.bfloat16)


def flux_body(
    use_slot,
    slot_row,
    table,
    weights,
    surf_temp,
    surf_hum,
    hum_factor,
    log_mom,
    cell_weight,
    rows_out,
    slot_sums,
    held,
    rows,
    contrib,
    in_sem,
    out_sem,
):
    blocks = held.shape[0]
    parts = blocks // FLUX_GROUP

    def fetch(p):
        share = pl.ds(pl.multiple_of(p * FLUX_GROUP, FLUX_GROUP), FLUX_GROUP)
        return pltpu.make_async_copy(weights.at[share], held.at[share], in_sem.at[p])

    def put(p):
        share = pl.ds(pl.multiple_of(p * (FLUX_GROUP * F), FLUX_GROUP * F), FLUX_GROUP * F)
        return pltpu.make_async_copy(rows.at[share], rows_out.at[share], out_sem.at[p])

    for p in range(parts):
        fetch(p).start()

    def part(p, _):
        base = p * FLUX_GROUP
        fetch(p).wait()
        for i in range(0, FLUX_GROUP, 2):
            k = base + i
            both = lax.dot_general(
                jnp.concatenate([table[use_slot[0, k]], table[use_slot[0, k + 1]]], axis=0),
                held[pl.ds(k, 2)].reshape(2 * BLK, ACELL),
                (((1,), (1,)), ((), ())),
                preferred_element_type=jnp.float32,
            )
            rows[pl.ds(pl.multiple_of(k * F, F), F), :] = both[:F, :BLK]
            rows[pl.ds(pl.multiple_of(k * F + F, F), F), :] = both[F:, BLK:]
        mine = pl.ds(pl.multiple_of(base, FLUX_GROUP), FLUX_GROUP)
        row = lambda f: pl.ds(base * F + f, FLUX_GROUP, stride=F)
        fluxes = flux_rows(
            *(rows[row(f), :] for f in range(4)),
            surf_temp[mine, :],
            surf_hum[mine, :],
            hum_factor[mine, :],
            log_mom[mine, :],
        )
        weight = cell_weight[mine, :]
        for f in range(4):
            rows[row(f), :] = weight * fluxes[f]
        put(p).start()
        for i in range(0, FLUX_GROUP, 2):
            k = base + i
            left = jnp.concatenate(
                [
                    rows[pl.ds(pl.multiple_of(k * F, F), 8), :],
                    rows[pl.ds(pl.multiple_of(k * F + F, F), 8), :],
                ],
                axis=0,
            ).astype(jnp.bfloat16)
            both = product(left, jnp.concatenate([held[k], held[k + 1]], axis=1))
            contrib[pl.ds(pl.multiple_of(k * 8, 8), 8), :] = both[:8, :ACELL]
            contrib[pl.ds(pl.multiple_of(k * 8 + 8, 8), 8), :] = both[8:, ACELL:]
        return 0

    lax.fori_loop(0, parts, part, 0)
    sum_rows(one_hot(slot_row[...], table.shape[0]), contrib, slot_sums, 8)
    for p in range(parts):
        put(p).wait()


def fluxes_of(slot_row, table, weights, cells):
    blocks = weights.shape[0]
    here = pl.BlockSpec(memory_space=VMEM)
    far = pl.BlockSpec(memory_space=pltpu.HBM)
    return pl.pallas_call(
        flux_body,
        out_shape=(
            pltpu.HBM((blocks * F, BLK), jnp.float32),
            jax.ShapeDtypeStruct((table.shape[0] * 4, ACELL), jnp.float32),
        ),
        in_specs=[pl.BlockSpec(memory_space=SMEM), here, here, far] + [here] * 5,
        out_specs=(far, here),
        scratch_shapes=[
            pltpu.VMEM(weights.shape, weights.dtype),
            pltpu.VMEM((blocks * F, BLK), jnp.float32),
            pltpu.VMEM((blocks * 8, ACELL), jnp.float32),
            pltpu.SemaphoreType.DMA((blocks // FLUX_GROUP,)),
            pltpu.SemaphoreType.DMA((blocks // FLUX_GROUP,)),
        ],
        compiler_params=pltpu.CompilerParams(vmem_limit_bytes=30 * MIB),
        name="fluxes",
    )(
        slot_row,
        slot_row,
        table,
        pltpu.with_memory_space_constraint(weights, pltpu.HBM),
        *cells,
    )


def ocean_body(ocean_block, rows_far, hot_far, passive_weight, ocean_sums, rows, hot, partial, sem):
    parts = hot.shape[0] // GROUP

    def fetch(p):
        flat = pl.ds(pl.multiple_of(p * (GROUP * F), GROUP * F), GROUP * F)
        share = pl.ds(pl.multiple_of(p * GROUP, GROUP), GROUP)
        return (
            pltpu.make_async_copy(rows_far.at[flat], rows.at[flat], sem.at[p]),
            pltpu.make_async_copy(hot_far.at[share], hot.at[share], sem.at[parts + p]),
        )

    for p in range(parts):
        for copy in fetch(p):
            copy.start()
    ocean_sums[...] = jnp.zeros_like(ocean_sums)
    is_flux = lax.broadcasted_iota(jnp.int32, (8, BLK), 0) < 4

    def part(p, _):
        for copy in fetch(p):
            copy.wait()
        for i in range(GROUP):
            k = p * GROUP + i
            factor = passive_weight[pl.ds(k, 1), :]
            value = rows[pl.ds(pl.multiple_of(k * F, F), F), :]
            value = jnp.concatenate(
                [jnp.where(is_flux, value[:8], value[:8] * factor), value[8:] * factor], axis=0
            )
            both = product(jnp.concatenate(two_parts(value), axis=0), hot[k])
            partial[i * F : (i + 1) * F, :] = both[:F] + both[F:]
        for i in range(GROUP):
            target = ocean_block[0, p * GROUP + i]
            ocean_sums[target] = ocean_sums[target] + partial[i * F : (i + 1) * F, :]
        return 0

    lax.fori_loop(0, parts, part, 0)


def ocean_of(block_row, rows, hot, passive_weight, owners):
    here = pl.BlockSpec(memory_space=VMEM)
    far = pl.BlockSpec(memory_space=pltpu.HBM)
    return pl.pallas_call(
        ocean_body,
        out_shape=jax.ShapeDtypeStruct((owners, F, OCELL), jnp.float32),
        in_specs=[pl.BlockSpec(memory_space=SMEM), far, far, here],
        out_specs=here,
        scratch_shapes=[
            pltpu.VMEM(rows.shape, rows.dtype),
            pltpu.VMEM(hot.shape, hot.dtype),
            pltpu.VMEM((GROUP * F, OCELL), jnp.float32),
            pltpu.SemaphoreType.DMA((2 * (hot.shape[0] // GROUP),)),
        ],
        compiler_params=pltpu.CompilerParams(vmem_limit_bytes=28 * MIB),
        cost_estimate=pl.CostEstimate(
            flops=128 * rows.size, bytes_accessed=12 * rows.size, transcendentals=0
        ),
        name="ocean",
    )(
        block_row,
        pltpu.with_memory_space_constraint(rows, pltpu.HBM),
        pltpu.with_memory_space_constraint(hot, pltpu.HBM),
        passive_weight,
    )


def owner_body(request_row, returned, ocean_sums, out):
    sum_rows(one_hot(request_row[...], out.shape[0] // 4), returned, out, 4)


def owner_sums_of(request_row, returned, ocean_sums, local_blocks):
    here = pl.BlockSpec(memory_space=VMEM)
    return pl.pallas_call(
        owner_body,
        out_shape=jax.ShapeDtypeStruct((local_blocks * 4, ACELL), jnp.float32),
        in_specs=[here, here, pl.BlockSpec(memory_space=pl.ANY)],
        out_specs=here,
        compiler_params=pltpu.CompilerParams(vmem_limit_bytes=8 * MIB),
        name="owner_sums",
    )(request_row, returned, ocean_sums)


def add_body(left, right, out):
    out[...] = left[...] + right[...]


def add(left, right):
    here = pl.BlockSpec(memory_space=VMEM)
    return pl.pallas_call(
        add_body,
        out_shape=jax.ShapeDtypeStruct(left.shape, left.dtype),
        in_specs=[here, here],
        out_specs=here,
        compiler_params=pltpu.CompilerParams(vmem_limit_bytes=8 * MIB),
        cost_estimate=ADD_COST,
        name="add",
    )(left, right)


def sum_over_ring(x, axis, other):
    ranks, places = lax.axis_size(axis), lax.axis_size(other)
    bit = 1
    while bit < ranks:
        mask = ranks - 1 if 2 * bit == ranks else bit

        def partner(i, turn):
            return (((i - turn) % ranks) ^ mask) + turn

        pairs = [
            (i * places + p, partner(i, (p % 2) * (ranks // 4)) % ranks * places + p)
            for i in range(ranks)
            for p in range(places)
        ]
        x = add(x, lax.ppermute(x, (axis, other), pairs))
        bit *= 2
    return x


def per_device(
    atm_fields,
    weights,
    surf_temp,
    surf_hum,
    roughness,
    cell_area,
    need_list,
    use_slot,
    ocean_block,
    ocean_cell,
    cell_count,
    ice_mask,
):
    owners = lax.axis_size("atm")
    local_blocks = atm_fields.shape[0]
    requests = lax.all_to_all(need_list[0], "atm", split_axis=0, concat_axis=0, tiled=True)
    table = lax.all_to_all(serve(requests, atm_fields), "atm", split_axis=0, concat_axis=0, tiled=True)
    hot, surf_temp, surf_hum, request_row = prep(ocean_cell, surf_temp, surf_hum, requests)
    ice_frac = ice_mask.astype(jnp.float32)
    is_live = jnp.arange(BLK, dtype=jnp.int32)[None, :] < cell_count[:, None]
    cell_weight = jnp.where(is_live, cell_area, 0.0)
    log_mom = jnp.log(ref_height / roughness)
    cells = (surf_temp, surf_hum, 1.0 - 0.6 * ice_frac, log_mom, cell_weight)
    passive_weight = cell_weight * (1.0 - 0.7 * ice_frac)
    rows, slot_sums = fluxes_of(use_slot.reshape(1, -1), table, weights, cells)
    returned = lax.all_to_all(slot_sums, "atm", split_axis=0, concat_axis=0, tiled=True)
    ocean_sums = ocean_of(ocean_block.reshape(1, -1), rows, hot, passive_weight, owners)
    owner_sums = owner_sums_of(request_row, returned, ocean_sums, local_blocks)
    ocean_parts = lax.all_to_all(ocean_sums, "atm", split_axis=0, concat_axis=0, tiled=True)
    atm_flux = sum_over_ring(owner_sums, "ocn", "atm").reshape(local_blocks, 4, ACELL)
    ocean_flux = jnp.sum(ocean_parts, axis=0, keepdims=True)
    return (atm_flux, ocean_flux)


def solution(mesh):
    placed = (
        P("atm", None, None),
        P(("ocn", "atm"), None, None),
        P(("ocn", "atm"), None),
        P(("ocn", "atm"), None),
        P(("ocn", "atm"), None),
        P(("ocn", "atm"), None),
        P(("ocn", "atm"), None, None),
        P(("ocn", "atm")),
        P(("ocn", "atm")),
        P(("ocn", "atm"), None),
        P(("ocn", "atm")),
        P(("ocn", "atm"), None),
    )
    return jax.shard_map(
        per_device,
        mesh=mesh,
        in_specs=placed,
        out_specs=(P("atm", None, None), P(("ocn", "atm"), None, None)),
        check_vma=False,
    )
```

```python
import math

import jax
import jax.numpy as jnp
from jax import lax
from jax.experimental import pallas as pl
from jax.experimental.pallas import tpu as pltpu
from jax.sharding import PartitionSpec as P

F = 32
BLK = 128
ACELL = 128
OCELL = 128
CAP = 4
ITERS = 8

ref_height = 10.0
karman = 0.4
buoyancy = 0.5
flux_scale = 40.0

GROUP = 64
FLUX_GROUP = 96
MIB = 1 << 20
ADD_COST = pl.CostEstimate(flops=1500000000, bytes_accessed=3 << 17, transcendentals=0)
VMEM = pltpu.VMEM
SMEM = pltpu.SMEM

ARCTAN = (
    0.9999999952,
    -0.3333319239,
    0.1999324926,
    -0.1416585733,
    0.1012280370,
    -0.0507783010,
)


def arctan_half(t):
    z = t * t
    total = jnp.full_like(z, ARCTAN[-1])
    for c in ARCTAN[-2::-1]:
        total = total * z + c
    return total * t


def flux_rows(mapped_u, mapped_v, mapped_t, mapped_q, surf_temp, surf_hum, hum_factor, log_mom):
    wind_u = 6.0 * mapped_u
    wind_v = 6.0 * mapped_v
    square_speed = wind_u * wind_u + wind_v * wind_v + 1.0
    wind_speed = jnp.sqrt(square_speed)
    temp_diff = mapped_t - surf_temp
    hum_diff = (mapped_q - surf_hum) * hum_factor
    log_heat = log_mom + math.log(10.0)
    gain = (ref_height * buoyancy) * (temp_diff + 0.2 * hum_diff) / square_speed
    from_mom = log_mom
    from_heat = log_heat
    for sweep in range(ITERS):
        stability = jnp.clip(gain * from_mom * from_mom / from_heat, -5.0, 1.0)
        unstable = jnp.minimum(stability, 0.0)
        square = jnp.sqrt(1.0 - 16.0 * unstable)
        root = jnp.sqrt(square)
        half_square = 0.5 + 0.5 * square
        half_root = 0.5 + 0.5 * root
        log_square = jnp.log(half_square)
        log_both = jnp.log(half_root * half_root * half_square)
        turn = arctan_half((root - 1.0) / (root + 1.0))
        stable = stability >= 0.0
        psi_stable = -5.0 * stability
        psi_mom = jnp.where(stable, psi_stable, log_both - 2.0 * turn)
        psi_heat = jnp.where(stable, psi_stable, 2.0 * log_square)
        from_mom = log_mom - psi_mom
        from_heat = log_heat - psi_heat
    fric_vel = karman * wind_speed / from_mom
    drag = flux_scale * fric_vel * fric_vel / wind_speed
    carry = -flux_scale * karman * fric_vel / from_heat
    return drag * wind_u, drag * wind_v, carry * temp_diff, carry * hum_diff


def serve_body(requests, fields, out):
    def owner(d, _):
        for c in range(CAP):
            out[d * CAP + c] = fields[requests[d, c]]
        return 0

    lax.fori_loop(0, out.shape[0] // CAP, owner, 0)


def serve(requests, fields):
    return pl.pallas_call(
        serve_body,
        out_shape=jax.ShapeDtypeStruct((requests.size,) + fields.shape[1:], fields.dtype),
        in_specs=[pl.BlockSpec(memory_space=SMEM), pl.BlockSpec(memory_space=VMEM)],
        out_specs=pl.BlockSpec(memory_space=VMEM),
        compiler_params=pltpu.CompilerParams(vmem_limit_bytes=8 * MIB),
        name="serve",
    )(requests, fields)


def prep_body(ocean_cell, surf_temp, surf_hum, requests, hot, temp, hum, request_row):
    request_row[...] = requests[...]
    temp[...] = surf_temp[...]
    hum[...] = surf_hum[...]
    target = lax.broadcasted_iota(jnp.int32, (OCELL, BLK), 0)
    for i in range(hot.shape[0]):
        hot[i] = jnp.where(target == ocean_cell[i : i + 1, :], 1.0, 0.0).astype(jnp.bfloat16).T


def prep(ocean_cell, surf_temp, surf_hum, requests):
    blocks = ocean_cell.shape[0]
    part = pl.BlockSpec((GROUP, BLK), lambda s: (s, 0))
    flat = jax.ShapeDtypeStruct((blocks, BLK), jnp.float32)
    line = pl.BlockSpec((1, requests.size), lambda s: (0, 0))
    return pl.pallas_call(
        prep_body,
        out_shape=(pltpu.HBM((blocks, BLK, OCELL), jnp.bfloat16), flat, flat, jax.ShapeDtypeStruct((1, requests.size), jnp.int32)),
        grid=(blocks // GROUP,),
        in_specs=[part] * 3 + [line],
        out_specs=(pl.BlockSpec((GROUP, BLK, OCELL), lambda s: (s, 0, 0)), part, part, line),
        compiler_params=pltpu.CompilerParams(vmem_limit_bytes=16 * MIB),
        cost_estimate=pl.CostEstimate(
            flops=2 * blocks * BLK * OCELL,
            bytes_accessed=2 * blocks * BLK * OCELL,
            transcendentals=0,
        ),
        name="prep",
    )(ocean_cell, surf_temp, surf_hum, requests.reshape(1, -1))


def two_parts(value):
    high = value.astype(jnp.bfloat16)
    return high, (value - high.astype(jnp.float32)).astype(jnp.bfloat16)


def product(left, right):
    return jnp.dot(left, right, preferred_element_type=jnp.float32)


def sum_rows(picked, values, out, stride):
    entries = picked.shape[1]
    for c in range(4):
        high, low = two_parts(values[pl.ds(c, entries, stride=stride), :])
        out[pl.ds(c, picked.shape[0], stride=4), :] = product(picked, high) + product(picked, low)


def one_hot(index_row, count):
    rows = lax.broadcasted_iota(jnp.int32, (count, index_row.shape[1]), 0)
    return jnp.where(rows == index_row, 1.0, 0.0).astype(jnp.bfloat16)


def flux_body(
    use_slot,
    slot_row,
    table,
    weights,
    surf_temp,
    surf_hum,
    hum_factor,
    log_mom,
    cell_weight,
    rows_out,
    slot_sums,
    held,
    rows,
    contrib,
    in_sem,
    out_sem,
):
    blocks = held.shape[0]
    parts = blocks // FLUX_GROUP

    def fetch(p):
        share = pl.ds(pl.multiple_of(p * FLUX_GROUP, FLUX_GROUP), FLUX_GROUP)
        return pltpu.make_async_copy(weights.at[share], held.at[share], in_sem.at[p])

    def put(p):
        share = pl.ds(pl.multiple_of(p * (FLUX_GROUP * F), FLUX_GROUP * F), FLUX_GROUP * F)
        return pltpu.make_async_copy(rows.at[share], rows_out.at[share], out_sem.at[p])

    for p in range(parts):
        fetch(p).start()

    def part(p, _):
        base = p * FLUX_GROUP
        fetch(p).wait()
        for i in range(0, FLUX_GROUP, 2):
            k = base + i
            both = lax.dot_general(
                jnp.concatenate([table[use_slot[0, k]], table[use_slot[0, k + 1]]], axis=0),
                held[pl.ds(k, 2)].reshape(2 * BLK, ACELL),
                (((1,), (1,)), ((), ())),
                preferred_element_type=jnp.float32,
            )
            rows[pl.ds(pl.multiple_of(k * F, F), F), :] = both[:F, :BLK]
            rows[pl.ds(pl.multiple_of(k * F + F, F), F), :] = both[F:, BLK:]
        mine = pl.ds(pl.multiple_of(base, FLUX_GROUP), FLUX_GROUP)
        row = lambda f: pl.ds(base * F + f, FLUX_GROUP, stride=F)
        fluxes = flux_rows(
            *(rows[row(f), :] for f in range(4)),
            surf_temp[mine, :],
            surf_hum[mine, :],
            hum_factor[mine, :],
            log_mom[mine, :],
        )
        weight = cell_weight[mine, :]
        for f in range(4):
            rows[row(f), :] = weight * fluxes[f]
        put(p).start()
        for i in range(0, FLUX_GROUP, 2):
            k = base + i
            left = jnp.concatenate(
                [
                    rows[pl.ds(pl.multiple_of(k * F, F), 8), :],
                    rows[pl.ds(pl.multiple_of(k * F + F, F), 8), :],
                ],
                axis=0,
            ).astype(jnp.bfloat16)
            both = product(left, jnp.concatenate([held[k], held[k + 1]], axis=1))
            contrib[pl.ds(pl.multiple_of(k * 8, 8), 8), :] = both[:8, :ACELL]
            contrib[pl.ds(pl.multiple_of(k * 8 + 8, 8), 8), :] = both[8:, ACELL:]
        return 0

    lax.fori_loop(0, parts, part, 0)
    sum_rows(one_hot(slot_row[...], table.shape[0]), contrib, slot_sums, 8)
    for p in range(parts):
        put(p).wait()


def fluxes_of(slot_row, table, weights, cells):
    blocks = weights.shape[0]
    here = pl.BlockSpec(memory_space=VMEM)
    far = pl.BlockSpec(memory_space=pltpu.HBM)
    return pl.pallas_call(
        flux_body,
        out_shape=(
            pltpu.HBM((blocks * F, BLK), jnp.float32),
            jax.ShapeDtypeStruct((table.shape[0] * 4, ACELL), jnp.float32),
        ),
        in_specs=[pl.BlockSpec(memory_space=SMEM), here, here, far] + [here] * 5,
        out_specs=(far, here),
        scratch_shapes=[
            pltpu.VMEM(weights.shape, weights.dtype),
            pltpu.VMEM((blocks * F, BLK), jnp.float32),
            pltpu.VMEM((blocks * 8, ACELL), jnp.float32),
            pltpu.SemaphoreType.DMA((blocks // FLUX_GROUP,)),
            pltpu.SemaphoreType.DMA((blocks // FLUX_GROUP,)),
        ],
        compiler_params=pltpu.CompilerParams(vmem_limit_bytes=30 * MIB),
        name="fluxes",
    )(
        slot_row,
        slot_row,
        table,
        pltpu.with_memory_space_constraint(weights, pltpu.HBM),
        *cells,
    )


def ocean_body(ocean_block, rows_far, hot_far, passive_weight, ocean_sums, rows, hot, partial, sem):
    parts = hot.shape[0] // GROUP

    def fetch(p):
        flat = pl.ds(pl.multiple_of(p * (GROUP * F), GROUP * F), GROUP * F)
        share = pl.ds(pl.multiple_of(p * GROUP, GROUP), GROUP)
        return (
            pltpu.make_async_copy(rows_far.at[flat], rows.at[flat], sem.at[p]),
            pltpu.make_async_copy(hot_far.at[share], hot.at[share], sem.at[parts + p]),
        )

    for p in range(parts):
        for copy in fetch(p):
            copy.start()
    ocean_sums[...] = jnp.zeros_like(ocean_sums)
    is_flux = lax.broadcasted_iota(jnp.int32, (8, BLK), 0) < 4

    def part(p, _):
        for copy in fetch(p):
            copy.wait()
        for i in range(GROUP):
            k = p * GROUP + i
            factor = passive_weight[pl.ds(k, 1), :]
            value = rows[pl.ds(pl.multiple_of(k * F, F), F), :]
            value = jnp.concatenate(
                [jnp.where(is_flux, value[:8], value[:8] * factor), value[8:] * factor], axis=0
            )
            both = product(jnp.concatenate(two_parts(value), axis=0), hot[k])
            partial[i * F : (i + 1) * F, :] = both[:F] + both[F:]
        for i in range(GROUP):
            target = ocean_block[0, p * GROUP + i]
            ocean_sums[target] = ocean_sums[target] + partial[i * F : (i + 1) * F, :]
        return 0

    lax.fori_loop(0, parts, part, 0)


def ocean_of(block_row, rows, hot, passive_weight, owners):
    here = pl.BlockSpec(memory_space=VMEM)
    far = pl.BlockSpec(memory_space=pltpu.HBM)
    return pl.pallas_call(
        ocean_body,
        out_shape=jax.ShapeDtypeStruct((owners, F, OCELL), jnp.float32),
        in_specs=[pl.BlockSpec(memory_space=SMEM), far, far, here],
        out_specs=here,
        scratch_shapes=[
            pltpu.VMEM(rows.shape, rows.dtype),
            pltpu.VMEM(hot.shape, hot.dtype),
            pltpu.VMEM((GROUP * F, OCELL), jnp.float32),
            pltpu.SemaphoreType.DMA((2 * (hot.shape[0] // GROUP),)),
        ],
        compiler_params=pltpu.CompilerParams(vmem_limit_bytes=28 * MIB),
        cost_estimate=pl.CostEstimate(
            flops=128 * rows.size, bytes_accessed=12 * rows.size, transcendentals=0
        ),
        name="ocean",
    )(
        block_row,
        pltpu.with_memory_space_constraint(rows, pltpu.HBM),
        pltpu.with_memory_space_constraint(hot, pltpu.HBM),
        passive_weight,
    )


def owner_body(request_row, returned, ocean_sums, out):
    sum_rows(one_hot(request_row[...], out.shape[0] // 4), returned, out, 4)


def owner_sums_of(request_row, returned, ocean_sums, local_blocks):
    here = pl.BlockSpec(memory_space=VMEM)
    return pl.pallas_call(
        owner_body,
        out_shape=jax.ShapeDtypeStruct((local_blocks * 4, ACELL), jnp.float32),
        in_specs=[here, here, pl.BlockSpec(memory_space=pl.ANY)],
        out_specs=here,
        compiler_params=pltpu.CompilerParams(vmem_limit_bytes=8 * MIB),
        name="owner_sums",
    )(request_row, returned, ocean_sums)


def add_body(left, right, out):
    out[...] = left[...] + right[...]


def add(left, right):
    here = pl.BlockSpec(memory_space=VMEM)
    return pl.pallas_call(
        add_body,
        out_shape=jax.ShapeDtypeStruct(left.shape, left.dtype),
        in_specs=[here, here],
        out_specs=here,
        compiler_params=pltpu.CompilerParams(vmem_limit_bytes=8 * MIB),
        cost_estimate=ADD_COST,
        name="add",
    )(left, right)


def sum_over_ring(x, axis, other):
    ranks, places = lax.axis_size(axis), lax.axis_size(other)
    masks = [ranks - 1] + [1 << bit for bit in range(ranks.bit_length() - 2)]
    for mask in masks:

        def partner(i, turn):
            return (((i - turn) % ranks) ^ mask) + turn

        pairs = [
            (i * places + p, partner(i, (p % 2) * (ranks // 4)) % ranks * places + p)
            for i in range(ranks)
            for p in range(places)
        ]
        x = add(x, lax.ppermute(x, (axis, other), pairs))
    return x


def per_device(
    atm_fields,
    weights,
    surf_temp,
    surf_hum,
    roughness,
    cell_area,
    need_list,
    use_slot,
    ocean_block,
    ocean_cell,
    cell_count,
    ice_mask,
):
    owners = lax.axis_size("atm")
    local_blocks = atm_fields.shape[0]
    requests = lax.all_to_all(need_list[0], "atm", split_axis=0, concat_axis=0, tiled=True)
    table = lax.all_to_all(serve(requests, atm_fields), "atm", split_axis=0, concat_axis=0, tiled=True)
    hot, surf_temp, surf_hum, request_row = prep(ocean_cell, surf_temp, surf_hum, requests)
    ice_frac = ice_mask.astype(jnp.float32)
    is_live = jnp.arange(BLK, dtype=jnp.int32)[None, :] < cell_count[:, None]
    cell_weight = jnp.where(is_live, cell_area, 0.0)
    log_mom = jnp.log(ref_height / roughness)
    cells = (surf_temp, surf_hum, 1.0 - 0.6 * ice_frac, log_mom, cell_weight)
    passive_weight = cell_weight * (1.0 - 0.7 * ice_frac)
    rows, slot_sums = fluxes_of(use_slot.reshape(1, -1), table, weights, cells)
    returned = lax.all_to_all(slot_sums, "atm", split_axis=0, concat_axis=0, tiled=True)
    ocean_sums = ocean_of(ocean_block.reshape(1, -1), rows, hot, passive_weight, owners)
    owner_sums = owner_sums_of(request_row, returned, ocean_sums, local_blocks)
    ocean_parts = lax.all_to_all(ocean_sums, "atm", split_axis=0, concat_axis=0, tiled=True)
    atm_flux = sum_over_ring(owner_sums, "ocn", "atm").reshape(local_blocks, 4, ACELL)
    ocean_flux = jnp.sum(ocean_parts, axis=0, keepdims=True)
    return (atm_flux, ocean_flux)


def solution(mesh):
    placed = (
        P("atm", None, None),
        P(("ocn", "atm"), None, None),
        P(("ocn", "atm"), None),
        P(("ocn", "atm"), None),
        P(("ocn", "atm"), None),
        P(("ocn", "atm"), None),
        P(("ocn", "atm"), None, None),
        P(("ocn", "atm")),
        P(("ocn", "atm")),
        P(("ocn", "atm"), None),
        P(("ocn", "atm")),
        P(("ocn", "atm"), None),
    )
    return jax.shard_map(
        per_device,
        mesh=mesh,
        in_specs=placed,
        out_specs=(P("atm", None, None), P(("ocn", "atm"), None, None)),
        check_vma=False,
    )
```

```python
import math

import jax
import jax.numpy as jnp
from jax import lax
from jax.experimental import pallas as pl
from jax.experimental.pallas import tpu as pltpu
from jax.sharding import PartitionSpec as P

F = 32
BLK = 128
ACELL = 128
OCELL = 128
CAP = 4
ITERS = 8

ref_height = 10.0
karman = 0.4
buoyancy = 0.5
flux_scale = 40.0

GROUP = 64
FLUX_PARTS = (32,96,128,128)
MIB = 1 << 20
ADD_COST = pl.CostEstimate(flops=1500000000, bytes_accessed=3 << 17, transcendentals=0)
VMEM = pltpu.VMEM
SMEM = pltpu.SMEM

ARCTAN = (
    0.9999999952,
    -0.3333319239,
    0.1999324926,
    -0.1416585733,
    0.1012280370,
    -0.0507783010,
)


def arctan_half(t):
    z = t * t
    total = jnp.full_like(z, ARCTAN[-1])
    for c in ARCTAN[-2::-1]:
        total = total * z + c
    return total * t


def flux_rows(mapped_u, mapped_v, mapped_t, mapped_q, surf_temp, surf_hum, hum_factor, log_mom):
    wind_u = 6.0 * mapped_u
    wind_v = 6.0 * mapped_v
    square_speed = wind_u * wind_u + wind_v * wind_v + 1.0
    wind_speed = jnp.sqrt(square_speed)
    temp_diff = mapped_t - surf_temp
    hum_diff = (mapped_q - surf_hum) * hum_factor
    log_heat = log_mom + math.log(10.0)
    gain = (ref_height * buoyancy) * (temp_diff + 0.2 * hum_diff) / square_speed
    from_mom = log_mom
    from_heat = log_heat
    for sweep in range(ITERS):
        stability = jnp.clip(gain * from_mom * from_mom / from_heat, -5.0, 1.0)
        unstable = jnp.minimum(stability, 0.0)
        square = jnp.sqrt(1.0 - 16.0 * unstable)
        root = jnp.sqrt(square)
        half_square = 0.5 + 0.5 * square
        half_root = 0.5 + 0.5 * root
        log_square = jnp.log(half_square)
        log_both = jnp.log(half_root * half_root * half_square)
        turn = arctan_half((root - 1.0) / (root + 1.0))
        stable = stability >= 0.0
        psi_stable = -5.0 * stability
        psi_mom = jnp.where(stable, psi_stable, log_both - 2.0 * turn)
        psi_heat = jnp.where(stable, psi_stable, 2.0 * log_square)
        from_mom = log_mom - psi_mom
        from_heat = log_heat - psi_heat
    fric_vel = karman * wind_speed / from_mom
    drag = flux_scale * fric_vel * fric_vel / wind_speed
    carry = -flux_scale * karman * fric_vel / from_heat
    return drag * wind_u, drag * wind_v, carry * temp_diff, carry * hum_diff


def serve_body(requests, fields_far, out_far, fields, out, in_sem, out_sem):
    quarters = out_sem.shape[0]
    owners = requests.shape[0] // quarters

    def put(q):
        share = pl.ds(q * owners * CAP, owners * CAP)
        return pltpu.make_async_copy(out.at[share], out_far.at[share], out_sem.at[q])

    fetch = pltpu.make_async_copy(fields_far, fields, in_sem)
    fetch.start()
    fetch.wait()
    for q in range(quarters):
        for d in range(q * owners, (q + 1) * owners):
            for c in range(CAP):
                out[d * CAP + c] = fields[requests[d, c]]
        put(q).start()
    for q in range(quarters):
        put(q).wait()


def serve(requests, fields):
    far = pl.BlockSpec(memory_space=pltpu.HBM)
    shape = (requests.size,) + fields.shape[1:]
    return pl.pallas_call(
        serve_body,
        out_shape=pltpu.HBM(shape, fields.dtype),
        in_specs=[pl.BlockSpec(memory_space=SMEM), far],
        out_specs=far,
        scratch_shapes=[
            pltpu.VMEM(fields.shape, fields.dtype),
            pltpu.VMEM(shape, fields.dtype),
            pltpu.SemaphoreType.DMA,
            pltpu.SemaphoreType.DMA((4,)),
        ],
        compiler_params=pltpu.CompilerParams(vmem_limit_bytes=8 * MIB),
        name="serve",
    )(requests, pltpu.with_memory_space_constraint(fields, pltpu.HBM))


def prep_body(ocean_cell, surf_temp, surf_hum, requests, hot, temp, hum, request_row):
    request_row[...] = requests[...]
    temp[...] = surf_temp[...]
    hum[...] = surf_hum[...]
    target = lax.broadcasted_iota(jnp.int32, (OCELL, BLK), 0)
    for i in range(hot.shape[0]):
        hot[i] = jnp.where(target == ocean_cell[i : i + 1, :], 1.0, 0.0).astype(jnp.bfloat16).T


def prep(ocean_cell, surf_temp, surf_hum, requests):
    blocks = ocean_cell.shape[0]
    part = pl.BlockSpec((GROUP, BLK), lambda s: (s, 0))
    flat = jax.ShapeDtypeStruct((blocks, BLK), jnp.float32)
    line = pl.BlockSpec((1, requests.size), lambda s: (0, 0))
    return pl.pallas_call(
        prep_body,
        out_shape=(pltpu.HBM((blocks, BLK, OCELL), jnp.bfloat16), flat, flat, jax.ShapeDtypeStruct((1, requests.size), jnp.int32)),
        grid=(blocks // GROUP,),
        in_specs=[part] * 3 + [line],
        out_specs=(pl.BlockSpec((GROUP, BLK, OCELL), lambda s: (s, 0, 0)), part, part, line),
        compiler_params=pltpu.CompilerParams(vmem_limit_bytes=16 * MIB),
        cost_estimate=pl.CostEstimate(
            flops=2 * blocks * BLK * OCELL,
            bytes_accessed=2 * blocks * BLK * OCELL,
            transcendentals=0,
        ),
        name="prep",
    )(ocean_cell, surf_temp, surf_hum, requests.reshape(1, -1))


def two_parts(value):
    high = value.astype(jnp.bfloat16)
    return high, (value - high.astype(jnp.float32)).astype(jnp.bfloat16)


def product(left, right):
    return jnp.dot(left, right, preferred_element_type=jnp.float32)


def sum_rows(picked, values, out, stride):
    entries = picked.shape[1]
    for c in range(4):
        high, low = two_parts(values[pl.ds(c, entries, stride=stride), :])
        out[pl.ds(c, picked.shape[0], stride=4), :] = product(picked, high) + product(picked, low)


def one_hot(index_row, count):
    rows = lax.broadcasted_iota(jnp.int32, (count, index_row.shape[1]), 0)
    return jnp.where(rows == index_row, 1.0, 0.0).astype(jnp.bfloat16)


def flux_body(
    use_slot,
    slot_row,
    table,
    weights,
    surf_temp,
    surf_hum,
    hum_factor,
    log_mom,
    cell_weight,
    rows_out,
    slot_sums,
    held,
    rows,
    contrib,
    in_sem,
    out_sem,
):
    firsts = [sum(FLUX_PARTS[:p]) for p in range(len(FLUX_PARTS))]

    def fetch(p):
        share = pl.ds(firsts[p], FLUX_PARTS[p])
        return pltpu.make_async_copy(weights.at[share], held.at[share], in_sem.at[p])

    def put(p):
        share = pl.ds(firsts[p] * F, FLUX_PARTS[p] * F)
        return pltpu.make_async_copy(rows.at[share], rows_out.at[share], out_sem.at[p])

    def map_pair(k):
        both = lax.dot_general(
            jnp.concatenate([table[use_slot[0, k]], table[use_slot[0, k + 1]]], axis=0),
            held[k : k + 2].reshape(2 * BLK, ACELL),
            (((1,), (1,)), ((), ())),
            preferred_element_type=jnp.float32,
        )
        rows[k * F : (k + 1) * F, :] = both[:F, :BLK]
        rows[(k + 1) * F : (k + 2) * F, :] = both[F:, BLK:]

    def contribute_pair(k):
        left = jnp.concatenate(
            [rows[k * F : k * F + 8, :], rows[(k + 1) * F : (k + 1) * F + 8, :]], axis=0
        ).astype(jnp.bfloat16)
        both = product(left, jnp.concatenate([held[k], held[k + 1]], axis=1))
        contrib[k * 8 : (k + 1) * 8, :] = both[:8, :ACELL]
        contrib[(k + 1) * 8 : (k + 2) * 8, :] = both[8:, ACELL:]

    def flux_part(p):
        mine = pl.ds(firsts[p], FLUX_PARTS[p])
        row = lambda f: pl.ds(firsts[p] * F + f, FLUX_PARTS[p], stride=F)
        fluxes = flux_rows(
            *(rows[row(f), :] for f in range(4)),
            surf_temp[mine, :],
            surf_hum[mine, :],
            hum_factor[mine, :],
            log_mom[mine, :],
        )
        weight = cell_weight[mine, :]
        for f in range(4):
            rows[row(f), :] = weight * fluxes[f]
        put(p).start()

    def pairs(p):
        return range(firsts[p], firsts[p] + FLUX_PARTS[p], 2)

    for p in range(len(FLUX_PARTS)):
        fetch(p).start()
    for p in range(len(FLUX_PARTS)):
        fetch(p).wait()
        for k in pairs(p):
            map_pair(k)
        flux_part(p)
        for k in pairs(p):
            contribute_pair(k)
    sum_rows(one_hot(slot_row[...], table.shape[0]), contrib, slot_sums, 8)
    for p in range(len(FLUX_PARTS)):
        put(p).wait()


def fluxes_of(slot_row, table, weights, cells):
    blocks = weights.shape[0]
    here = pl.BlockSpec(memory_space=VMEM)
    far = pl.BlockSpec(memory_space=pltpu.HBM)
    return pl.pallas_call(
        flux_body,
        out_shape=(
            pltpu.HBM((blocks * F, BLK), jnp.float32),
            jax.ShapeDtypeStruct((table.shape[0] * 4, ACELL), jnp.float32),
        ),
        in_specs=[pl.BlockSpec(memory_space=SMEM), here, here, far] + [here] * 5,
        out_specs=(far, here),
        scratch_shapes=[
            pltpu.VMEM(weights.shape, weights.dtype),
            pltpu.VMEM((blocks * F, BLK), jnp.float32),
            pltpu.VMEM((blocks * 8, ACELL), jnp.float32),
            pltpu.SemaphoreType.DMA((len(FLUX_PARTS),)),
            pltpu.SemaphoreType.DMA((len(FLUX_PARTS),)),
        ],
        compiler_params=pltpu.CompilerParams(vmem_limit_bytes=30 * MIB),
        name="fluxes",
    )(
        slot_row,
        slot_row,
        table,
        pltpu.with_memory_space_constraint(weights, pltpu.HBM),
        *cells,
    )


def ocean_body(ocean_block, rows_far, hot_far, passive_weight, ocean_sums, rows, hot, partial, sem):
    parts = hot.shape[0] // GROUP

    def fetch(p):
        flat = pl.ds(pl.multiple_of(p * (GROUP * F), GROUP * F), GROUP * F)
        share = pl.ds(pl.multiple_of(p * GROUP, GROUP), GROUP)
        return (
            pltpu.make_async_copy(rows_far.at[flat], rows.at[flat], sem.at[p]),
            pltpu.make_async_copy(hot_far.at[share], hot.at[share], sem.at[parts + p]),
        )

    for p in range(parts):
        for copy in fetch(p):
            copy.start()
    ocean_sums[...] = jnp.zeros_like(ocean_sums)
    is_flux = lax.broadcasted_iota(jnp.int32, (8, BLK), 0) < 4

    def part(p, _):
        for copy in fetch(p):
            copy.wait()
        for i in range(GROUP):
            k = p * GROUP + i
            factor = passive_weight[pl.ds(k, 1), :]
            value = rows[pl.ds(pl.multiple_of(k * F, F), F), :]
            value = jnp.concatenate(
                [jnp.where(is_flux, value[:8], value[:8] * factor), value[8:] * factor], axis=0
            )
            both = product(jnp.concatenate(two_parts(value), axis=0), hot[k])
            partial[i * F : (i + 1) * F, :] = both[:F] + both[F:]
        for i in range(GROUP):
            target = ocean_block[0, p * GROUP + i]
            ocean_sums[target] = ocean_sums[target] + partial[i * F : (i + 1) * F, :]
        return 0

    lax.fori_loop(0, parts, part, 0)


def ocean_of(block_row, rows, hot, passive_weight, owners):
    here = pl.BlockSpec(memory_space=VMEM)
    far = pl.BlockSpec(memory_space=pltpu.HBM)
    return pl.pallas_call(
        ocean_body,
        out_shape=jax.ShapeDtypeStruct((owners, F, OCELL), jnp.float32),
        in_specs=[pl.BlockSpec(memory_space=SMEM), far, far, here],
        out_specs=here,
        scratch_shapes=[
            pltpu.VMEM(rows.shape, rows.dtype),
            pltpu.VMEM(hot.shape, hot.dtype),
            pltpu.VMEM((GROUP * F, OCELL), jnp.float32),
            pltpu.SemaphoreType.DMA((2 * (hot.shape[0] // GROUP),)),
        ],
        compiler_params=pltpu.CompilerParams(vmem_limit_bytes=28 * MIB),
        cost_estimate=pl.CostEstimate(
            flops=128 * rows.size, bytes_accessed=12 * rows.size, transcendentals=0
        ),
        name="ocean",
    )(
        block_row,
        pltpu.with_memory_space_constraint(rows, pltpu.HBM),
        pltpu.with_memory_space_constraint(hot, pltpu.HBM),
        passive_weight,
    )


def owner_body(request_row, returned, ocean_sums, out):
    sum_rows(one_hot(request_row[...], out.shape[0] // 4), returned, out, 4)


def owner_sums_of(request_row, returned, ocean_sums, local_blocks):
    here = pl.BlockSpec(memory_space=VMEM)
    return pl.pallas_call(
        owner_body,
        out_shape=jax.ShapeDtypeStruct((local_blocks * 4, ACELL), jnp.float32),
        in_specs=[here, here, pl.BlockSpec(memory_space=pl.ANY)],
        out_specs=here,
        compiler_params=pltpu.CompilerParams(vmem_limit_bytes=8 * MIB),
        name="owner_sums",
    )(request_row, returned, ocean_sums)


def add_body(left, right, out):
    out[...] = left[...] + right[...]


def add(left, right):
    here = pl.BlockSpec(memory_space=VMEM)
    return pl.pallas_call(
        add_body,
        out_shape=jax.ShapeDtypeStruct(left.shape, left.dtype),
        in_specs=[here, here],
        out_specs=here,
        compiler_params=pltpu.CompilerParams(vmem_limit_bytes=8 * MIB),
        cost_estimate=ADD_COST,
        name="add",
    )(left, right)


def sum_over_ring(x, axis, other):
    ranks, places = lax.axis_size(axis), lax.axis_size(other)
    bit = 1
    while bit < ranks:
        mask = ranks - 1 if 2 * bit == ranks else bit

        def partner(i, turn):
            return (((i - turn) % ranks) ^ mask) + turn

        pairs = [
            (i * places + p, partner(i, (p % 2) * (ranks // 4)) % ranks * places + p)
            for i in range(ranks)
            for p in range(places)
        ]
        x = add(x, lax.ppermute(x, (axis, other), pairs))
        bit *= 2
    return x


def per_device(
    atm_fields,
    weights,
    surf_temp,
    surf_hum,
    roughness,
    cell_area,
    need_list,
    use_slot,
    ocean_block,
    ocean_cell,
    cell_count,
    ice_mask,
):
    owners = lax.axis_size("atm")
    local_blocks = atm_fields.shape[0]
    requests = lax.all_to_all(need_list[0], "atm", split_axis=0, concat_axis=0, tiled=True)
    table = lax.all_to_all(serve(requests, atm_fields), "atm", split_axis=0, concat_axis=0, tiled=True)
    hot, surf_temp, surf_hum, request_row = prep(ocean_cell, surf_temp, surf_hum, requests)
    ice_frac = ice_mask.astype(jnp.float32)
    is_live = jnp.arange(BLK, dtype=jnp.int32)[None, :] < cell_count[:, None]
    cell_weight = jnp.where(is_live, cell_area, 0.0)
    log_mom = jnp.log(ref_height / roughness)
    cells = (surf_temp, surf_hum, 1.0 - 0.6 * ice_frac, log_mom, cell_weight)
    passive_weight = cell_weight * (1.0 - 0.7 * ice_frac)
    rows, slot_sums = fluxes_of(use_slot.reshape(1, -1), table, weights, cells)
    returned = lax.all_to_all(slot_sums, "atm", split_axis=0, concat_axis=0, tiled=True)
    ocean_sums = ocean_of(ocean_block.reshape(1, -1), rows, hot, passive_weight, owners)
    owner_sums = owner_sums_of(request_row, returned, ocean_sums, local_blocks)
    ocean_parts = lax.all_to_all(ocean_sums, "atm", split_axis=0, concat_axis=0, tiled=True)
    atm_flux = sum_over_ring(owner_sums, "ocn", "atm").reshape(local_blocks, 4, ACELL)
    ocean_flux = jnp.sum(ocean_parts, axis=0, keepdims=True)
    return (atm_flux, ocean_flux)


def solution(mesh):
    placed = (
        P("atm", None, None),
        P(("ocn", "atm"), None, None),
        P(("ocn", "atm"), None),
        P(("ocn", "atm"), None),
        P(("ocn", "atm"), None),
        P(("ocn", "atm"), None),
        P(("ocn", "atm"), None, None),
        P(("ocn", "atm")),
        P(("ocn", "atm")),
        P(("ocn", "atm"), None),
        P(("ocn", "atm")),
        P(("ocn", "atm"), None),
    )
    return jax.shard_map(
        per_device,
        mesh=mesh,
        in_specs=placed,
        out_specs=(P("atm", None, None), P(("ocn", "atm"), None, None)),
        check_vma=False,
    )
```
